256 devices in a mesh: row: 64 (over z, y, x_hi), rep: 4 (over x_lo, core).
Axes of the slice: x: 4 (x_hi: 2, x_lo: 2; x = x_hi * 2 + x_lo), y: 4, z: 8, core: 2. Of those that a mesh axis runs over, the one named last changes fastest.
Arguments:
- features: float32 [65536, 256], P(('row', 'rep')), may hold values from -6 to 6
- weight: float32 [256, 256], replicated, may hold values from -0.375 to 0.375
- cotangent: float32 [65536, 256], P(('row', 'rep')), may hold values from -6 to 6
- tile_row: int32 [64, 4, 128], P('row', 'rep'), may hold values from 0 to 7
- tile_col: int32 [64, 4, 128], P('row', 'rep'), may hold values from 0 to 511, as said below
- tile_count: int32 [64, 4], P('row', 'rep'), may hold values from 2 to 128, as said below
- tile_values: float32 [64, 4, 128, 128, 128], P('row', 'rep'), may hold values from -0.09375 to 0.09375
Outputs:
- activation: float32 [65536, 256], P(('row', 'rep'))
- feature_grad: float32 [65536, 256], P(('row', 'rep'))
- weight_grad: float32 [256, 256], replicated
The draws below stay inside these ranges and needn't reach their ends.
Inputs may be any that keep to these rules, and one draw needn't show every extreme that they name: `tile_col`: for a tile of row block b with row tile t the column tile is (b * 8 + t + o) mod 512 with -16 <= o <= 16; every device's live slots hold both o = -16 and o = 16. Slots from tile_count on are ignored, whatever they hold; some device has exactly 128 live slots.
All inputs are finite; a program needn't handle non-finite values.
Results may differ from the reference program's by a relative error of at most 0.0003.
Values sent between devices are 32-bit elements; how exact they have to be, the bound alone decides.
A program may use at most 128 MiB of HBM per device.

```python
import jax
import jax.numpy as jnp
from jax import lax

F = 256
TILE = 128
TPB = 8
TCAP = 128
SPAN = 2
BLOCKS = 64
REPS = 4
NTILES = 512
NODES = 65536


def tile_layout(key):
    key_rows, key_offsets = jax.random.split(key)
    shape = (BLOCKS, REPS, TCAP)
    tile_rows = jax.random.randint(key_rows, shape, 0, TPB)
    offsets = jax.random.randint(key_offsets, shape, -SPAN * TPB, SPAN * TPB + 1)
    slot_index = jnp.arange(TCAP)[None, None, :]
    tile_rows = jnp.where(slot_index == 0, 0, jnp.where(slot_index == 1, TPB - 1, tile_rows))
    offsets = jnp.where(slot_index == 0, -SPAN * TPB, jnp.where(slot_index == 1, SPAN * TPB, offsets))
    block_start = jnp.arange(BLOCKS)[:, None, None] * TPB
    columns = jnp.mod(block_start + tile_rows + offsets, NTILES)
    return (tile_rows.astype(jnp.int32), columns.astype(jnp.int32))


def draw_tile_row(key, part):
    return tile_layout(key)[0]


def draw_tile_col(key, part):
    return tile_layout(key)[1]


def draw_tile_count(key, part):
    key = jax.random.fold_in(key, 3)
    key_counts, key_full = jax.random.split(key)
    counts = jax.random.randint(key_counts, (BLOCKS * REPS,), 2, TCAP + 1)
    chosen = jax.random.randint(key_full, (), 0, BLOCKS * REPS)
    counts = jnp.where(jnp.arange(BLOCKS * REPS) == chosen, TCAP, counts)
    return counts.reshape(BLOCKS, REPS).astype(jnp.int32)


def shard_levels(rng, dims, cuts, least, high):
    level = 1.0
    for position, blocks in cuts:
        draws = jax.random.uniform(jax.random.fold_in(jax.random.fold_in(rng, 6), position), (blocks,), jnp.float32, least / len(cuts), high / len(cuts))
        level = level * jnp.repeat(jnp.exp(draws), dims[position] // blocks).reshape((-1,) + (1,) * (len(dims) - 1 - position))
    return level


def scatter_about(stream_key, dims, deviation, bound, cuts=(), held_as=jnp.bfloat16):
    level = shard_levels(stream_key, dims, cuts, -0.22, 0.18) if cuts else 1.0
    entries = jax.random.normal(stream_key, dims, jnp.float32) * deviation * level
    return jnp.minimum(jnp.maximum(entries, -bound), bound).astype(held_as)


def setup_inputs(seed: int = 0) -> dict:
    keys = jax.random.split(jax.random.key(seed), 8)
    features = scatter_about(keys[0], (NODES, F), 1.0, 6.0, ((0, 256),), jnp.float32)
    weight = scatter_about(keys[1], (F, F), F ** -0.5, 0.375, (), jnp.float32)
    cotangent = scatter_about(keys[2], (NODES, F), 1.0, 6.0, ((0, 256),), jnp.float32)
    tile_row = draw_tile_row(jax.random.fold_in(keys[7], 71), 0)
    tile_col = draw_tile_col(jax.random.fold_in(keys[7], 71), 0)
    tile_count = draw_tile_count(jax.random.fold_in(keys[7], 71), 0)
    tile_values = scatter_about(keys[6], (BLOCKS, REPS, TCAP, TILE, TILE), (TILE * TCAP * REPS // (2 * TPB)) ** -0.5, 0.09375, ((0, 64), (1, 4)), jnp.float32)
    return dict(features=features, weight=weight, cotangent=cotangent, tile_row=tile_row, tile_col=tile_col, tile_count=tile_count, tile_values=tile_values)


def silu_slope(pre_act):
    sigma_value = jax.nn.sigmoid(pre_act)
    return sigma_value * (1.0 + pre_act * (1.0 - sigma_value))


def reference(features, weight, cotangent, tile_row, tile_col, tile_count, tile_values):
    precise = lax.Precision.HIGHEST
    node_count, feat_width = features.shape
    slot_count = tile_row.shape[2]
    tiled = features.reshape(node_count // TILE, TILE, feat_width)
    slot_ids = jnp.arange(slot_count, dtype=jnp.int32)
    row_ids = jnp.arange(TPB, dtype=jnp.int32)

    def forward_block(carry, items):
        rows_here, cols_here, count_here, values_here = items
        is_live = slot_ids[None, :] < count_here[:, None]
        gathered = tiled[cols_here]
        products = jnp.einsum("ptij,ptjf->ptif", values_here, gathered, precision=precise)
        row_hot = ((rows_here[:, :, None] == row_ids[None, None, :]) & is_live[:, :, None]).astype(jnp.float32)
        summed = jnp.einsum("ptb,ptif->bif", row_hot, products, precision=precise)
        return carry, summed

    unused, blocks_out = lax.scan(forward_block, jnp.zeros((), jnp.float32), (tile_row, tile_col, tile_count, tile_values))
    aggregated = blocks_out.reshape(node_count, feat_width)
    pre_act = jnp.dot(aggregated, weight, precision=precise, preferred_element_type=jnp.float32)
    activation = jax.nn.silu(pre_act)
    grad_pre = cotangent * silu_slope(pre_act)
    grad_agg = jnp.dot(grad_pre, weight.T, precision=precise, preferred_element_type=jnp.float32)
    weight_grad = jnp.dot(aggregated.T, grad_pre, precision=precise, preferred_element_type=jnp.float32)
    grad_blocks = grad_agg.reshape(node_count // (TPB * TILE), TPB, TILE, feat_width)

    def backward_block(carry, items):
        rows_here, cols_here, count_here, values_here, grad_here = items
        is_live = (slot_ids[None, :] < count_here[:, None]).astype(jnp.float32)
        picked = grad_here[rows_here]
        products = jnp.einsum("ptij,ptif->ptjf", values_here, picked, precision=precise)
        products = products * is_live[:, :, None, None]
        carry = carry.at[cols_here.reshape(-1)].add(products.reshape(-1, TILE, feat_width))
        return carry, jnp.zeros((), jnp.float32)

    start = jnp.zeros((node_count // TILE, TILE, feat_width), jnp.float32)
    feature_grad, unused_two = lax.scan(backward_block, start, (tile_row, tile_col, tile_count, tile_values, grad_blocks))
    return activation, feature_grad.reshape(node_count, feat_width), weight_grad
```

```python
import jax
import jax.numpy as jnp
from jax import lax
from jax.experimental import pallas as pl
from jax.experimental.pallas import tpu as pltpu
from jax.sharding import PartitionSpec as P

TILE = 128
TPB = 8
SPAN = 2
SLOTS = 128
F = 256
ROWS = 256
WIN = 20
BAND_TILES = 40
PLANE = 32
MESH = pl.DeviceIdType.MESH
F32 = jnp.float32
BF16 = jnp.bfloat16


def split(value):
    high = value.astype(BF16)
    low = (value - high.astype(F32)).astype(BF16)
    return high, low


def dot(a, b):
    return jnp.dot(a, b, preferred_element_type=F32)


def dot_t(a, b):
    return lax.dot_general(a, b, (((1,), (1,)), ((), ())), preferred_element_type=F32)


def dot3(op, a, b):
    ah, al = split(a)
    bh, bl = split(b)
    return op(ah, bh) + (op(al, bh) + op(ah, bl))


def choose(i, values):
    out = values[0]
    for k in range(1, len(values)):
        out = jnp.where(i == k, values[k], out)
    return out


def kernel(
    feat, weight, cot, tiles, perm, keep, place,
    act_out, fg_out, wg_out,
    tilebuf, run, dense_h, dense_l, win, acc, rs_in, rs_mid, rs_send, gt, gt_h, gt_l, mrecv, rbuf,
    wg_loc, ar_a, ar_b, wg_sum, cot_v, w_v,
    loc_sem, fs_sem, fr_sem, ms_sem, mr_sem, rs_s, rs_r, ag_s, ag_r, bm_s, bm_r, br_s, br_r,
    aa_s, aa_r, ab_s, ab_r, ac_s, ac_r,
):
    row = lax.axis_index("row")
    rep = lax.axis_index("rep")
    yy = lax.div(row, 2)
    xl = lax.div(rep, 2)
    c = lax.rem(rep, 2)
    xh = lax.rem(row, 2)
    x = xh * 2 + xl
    q = x + 1 - 2 * xl
    w = 3 - x
    o = lax.rem(x + 2, 4)
    h = 2 * xh - 1
    l = 1 - 2 * xh
    nyy = lax.axis_size("row") // 2

    def dev(xx, yv, cc):
        yv = lax.rem(yv + nyy, nyy)
        return (yv * 2 + lax.div(xx, 2), lax.rem(xx, 2) * 2 + cc)

    def slot(at, dyy, xx, cc):
        return (2 * dyy + lax.div(xx, 2) - lax.div(at, 2) + SPAN) * 4 + lax.rem(xx, 2) * 2 + cc

    mate = dev(x, yy, 1 - c)
    zi = lax.div(row, 8)
    nz = nyy // 4
    m_me = lax.rem(row, 8) * 4 + rep

    def plane_dev(m):
        return (zi * 8 + lax.div(m, 4), lax.rem(m, 4))

    def remote(src, dst, ssem, rsem, to):
        return pltpu.make_async_remote_copy(
            src_ref=src, dst_ref=dst, send_sem=ssem, recv_sem=rsem, device_id=to, device_id_type=MESH
        )

    tile_cp = pltpu.make_async_copy(tiles, tilebuf, loc_sem.at[0])
    tile_cp.start()
    own = slot(x, 0, x, c)
    feat_cp = pltpu.make_async_copy(feat, win.at[own], loc_sem.at[1])
    feat_cp.start()
    cot_cp = pltpu.make_async_copy(cot, cot_v, loc_sem.at[2])
    cot_cp.start()
    w_cp = pltpu.make_async_copy(weight, w_v, loc_sem.at[3])
    w_cp.start()

    bar = pltpu.get_barrier_semaphore()

    def greet(to):
        pl.semaphore_signal(bar, inc=1, device_id=to, device_id_type=MESH)

    @pl.loop(1, PLANE)
    def _(d):
        greet(plane_dev(lax.rem(m_me + d, PLANE)))

    @pl.loop(1, nz)
    def _(d):
        greet((lax.rem(row + 8 * d, nz * 8), rep))

    greet(dev(x, yy + 1, c))
    greet(dev(x, yy - 1, c))
    pl.semaphore_wait(bar, PLANE - 1 + nz - 1 + 2)

    sends = []

    def fsend(n, src, dst_slot, to):
        cp = remote(src, win.at[dst_slot], fs_sem.at[n], fr_sem.at[dst_slot], to)
        cp.start()
        sends.append(cp)

    def frecv(s):
        remote(feat, win.at[s], fs_sem.at[0], fr_sem.at[s], mate).wait_recv()

    fsend(0, feat, slot(q, 0, x, c), dev(q, yy, c))
    fsend(1, feat, slot(x, -1, x, c), dev(x, yy + 1, c))
    fsend(2, feat, slot(x, 1, x, c), dev(x, yy - 1, c))
    fsend(3, feat, slot(w, 0, x, c), dev(w, yy, c))
    fsend(4, feat, own, mate)

    acc[...] = jnp.zeros_like(acc)
    run[SLOTS] = jnp.zeros((TILE, TILE), F32)
    tile_cp.wait()

    def merge(t, prev):
        value = prev * keep[t] + tilebuf[perm[t]]
        run[t] = value
        return value

    lax.fori_loop(0, SLOTS, merge, jnp.zeros((TILE, TILE), F32))

    @pl.loop(0, WIN)
    def _(j):
        for r in range(TPB):
            for half in range(2):
                high, low = split(run[place[r * BAND_TILES + j * 2 + half]])
                dense_h[j, r * TILE:(r + 1) * TILE, half * TILE:(half + 1) * TILE] = high
                dense_l[j, r * TILE:(r + 1) * TILE, half * TILE:(half + 1) * TILE] = low

    feat_cp.wait()

    def forward(s):
        xh_, xl_ = split(win[s])
        a = dense_h[s]
        acc[...] += dot(a, xh_) + (dot(dense_l[s], xh_) + dot(a, xl_))

    def forward_group(slots):
        @pl.loop(0, len(slots))
        def _(i):
            forward(choose(i, slots))

    def forward_recv_group(slots):
        @pl.loop(0, len(slots))
        def _(i):
            s = choose(i, slots)
            frecv(s)
            forward(s)

    def flip(s):
        return s + 1 - 2 * c

    s_q, s_w = slot(x, 0, q, c), slot(x, 0, w, c)
    s_hx, s_lx = slot(x, h, x, c), slot(x, l, x, c)
    s_o, s_hw = slot(x, 0, o, c), slot(x, h, w, c)
    s_lq, s_hq = slot(x, l, q, c), slot(x, h, q, c)
    s_ho = slot(x, h, o, c)

    frecv(s_q)
    fsend(5, win.at[s_q], slot(w, 0, q, c), dev(w, yy, c))
    fsend(6, win.at[s_q], slot(x, l, q, c), dev(x, yy + h, c))
    frecv(s_w)
    fsend(7, win.at[s_w], slot(x, h, w, c), dev(x, yy - h, c))
    frecv(s_hx)
    qh_src = jnp.where(c == 0, s_hx, s_q)
    qh_dst = jnp.where(c == 0, slot(q, h, x, c), slot(x, h, q, c))
    to_q, to_y = dev(q, yy, c), dev(x, yy - h, c)
    qh_to = (jnp.where(c == 0, to_q[0], to_y[0]), jnp.where(c == 0, to_q[1], to_y[1]))
    fsend(8, win.at[qh_src], qh_dst, qh_to)
    frecv(s_lx)
    fsend(9, win.at[s_q], s_q, mate)
    fsend(10, win.at[s_w], s_w, mate)
    fsend(11, win.at[s_hx], s_hx, mate)
    fsend(12, win.at[s_lx], s_lx, mate)
    forward_group([own, s_q, s_w])
    frecv(s_hw)
    fsend(13, win.at[s_hw], slot(q, h, w, c), dev(q, yy, c))
    fsend(14, win.at[s_hw], s_hw, mate)
    forward_group([s_hx, s_lx])
    frecv(s_o)
    fsend(15, win.at[s_o], s_o, mate)
    frecv(s_lq)
    fsend(16, win.at[s_lq], s_lq, mate)
    frecv(s_hq)
    fsend(17, win.at[s_hq], s_hq, mate)
    forward_recv_group([flip(own), flip(s_q), flip(s_w), flip(s_hx), flip(s_lx), flip(s_hw)])
    forward_group([s_hw, s_o, s_lq, s_hq])
    frecv(s_ho)
    fsend(18, win.at[s_ho], s_ho, mate)
    forward_recv_group([flip(s_o), flip(s_lq), flip(s_hq)])
    forward_group([s_ho])
    forward_recv_group([flip(s_ho)])

    k_o = (1 - xl) * 2 + c
    k_m = xl * 2 + 1 - c
    k_mo = (1 - xl) * 2 + 1 - c

    def chunk(k):
        return acc.at[pl.ds(pl.multiple_of(k * ROWS, ROWS), ROWS)]

    rs0 = remote(chunk(k_mo), rs_in.at[0], rs_s.at[0], rs_r.at[0], mate)
    rs0.start()
    rs1 = remote(chunk(k_m), rs_in.at[1], rs_s.at[1], rs_r.at[1], mate)
    rs1.start()
    for cp in sends:
        cp.wait_send()
    cot_cp.wait()
    w_cp.wait()
    rs0.wait_recv()
    rs_send[...] = chunk(k_o)[...] + rs_in[0]
    rs2 = remote(rs_send, rs_mid, rs_s.at[2], rs_r.at[2], dev(q, yy, c))
    rs2.start()
    rs1.wait_recv()
    rs2.wait_recv()
    agg = chunk(rep)[...] + rs_in[1] + rs_mid[...]

    wv = w_v[...]
    pre = dot3(dot, agg, wv)
    sig = jax.nn.sigmoid(pre)
    act_out[...] = pre * sig
    gp = cot_v[...] * (sig * (1.0 + pre * (1.0 - sig)))
    gt[rep] = dot3(dot_t, wv, gp)

    ag0 = remote(gt.at[rep], gt.at[rep], ag_s.at[0], ag_r.at[rep], dev(q, yy, c))
    ag0.start()
    ag1 = remote(gt.at[rep], gt.at[rep], ag_s.at[1], ag_r.at[rep], mate)
    ag1.start()

    def grecv(k):
        remote(gt.at[k], gt.at[k], ag_s.at[0], ag_r.at[k], mate).wait_recv()

    wg = dot3(dot, agg.T, gp).reshape(PLANE, F // PLANE, F)
    wg_loc[...] = wg

    def ar_copy(d, src, dst, ssem, rsem):
        return remote(src, dst, ssem.at[d], rsem.at[d], plane_dev(lax.rem(m_me + d, PLANE)))

    def aa_copy(d):
        return ar_copy(d, wg_loc.at[lax.rem(m_me + d, PLANE)], ar_a.at[m_me], aa_s, aa_r)

    def ab_copy(d):
        return remote(wg_sum, ar_b.at[zi], ab_s.at[d], ab_r.at[d], (lax.rem(row + 8 * d, nz * 8), rep))

    def ac_copy(d):
        return ar_copy(d, wg_out.at[m_me], wg_out.at[m_me], ac_s, ac_r)

    @pl.loop(1, PLANE)
    def _(d):
        aa_copy(d).start()

    ar_a[m_me] = wg_loc[m_me]

    grecv(k_m)

    def spread(pair):
        for half in range(2):
            high, low = split(gt[pair * 2 + half])
            gt_h[pair, :, half * ROWS:(half + 1) * ROWS] = high
            gt_l[pair, :, half * ROWS:(half + 1) * ROWS] = low

    def backward(s, pair):
        rows = pl.ds(pl.multiple_of(pair * 2 * ROWS, 2 * ROWS), 2 * ROWS)
        a = dense_h[s, rows, :]
        g = gt_h[pair]
        return dot(g, a) + (dot(gt_l[pair], a) + dot(g, dense_l[s, rows, :]))

    spread(xl)

    def first_pass(begin, end):
        @pl.loop(begin, end)
        def _(s):
            win[s] = backward(s, xl)

    first_pass(0, 12)
    grecv(k_o)
    ag2 = remote(gt.at[k_o], gt.at[k_o], ag_s.at[2], ag_r.at[k_o], mate)
    ag2.start()

    @pl.loop(1, PLANE)
    def _(d):
        aa_copy(d).wait_recv()

    total = ar_a[0]
    for k in range(1, PLANE):
        total = total + ar_a[k]
    wg_sum[...] = total
    ar_b[zi] = total

    @pl.loop(1, nz)
    def _(d):
        ab_copy(d).start()

    first_pass(12, WIN)
    grecv(k_mo)
    spread(1 - xl)

    @pl.loop(1, nz)
    def _(d):
        ab_copy(d).wait_recv()

    total = ar_b[0]
    for k in range(1, nz):
        total = total + ar_b[k]
    wg_out[m_me] = total

    @pl.loop(1, PLANE)
    def _(d):
        ac_copy(d).start()

    def mate_copy(s):
        i = lax.div(s, 2)
        return remote(win.at[s], mrecv.at[i], bm_s.at[i], bm_r.at[i], mate)

    def second_pass(slots):
        @pl.loop(0, len(slots))
        def _(i):
            s = choose(i, slots)
            other = flip(s)
            win[other] += backward(other, 1 - xl)
            mate_copy(other).start()
            win[s] += backward(s, 1 - xl)

    def add_mate(s):
        mate_copy(s).wait_recv()
        win[s] += mrecv[lax.div(s, 2)]

    back = []

    def bsend(n, s, to):
        cp = remote(win.at[s], rbuf.at[n], br_s.at[n], br_r.at[n], to)
        cp.start()
        back.append(cp)

    def badd(n, s):
        back[n].wait_recv()
        win[s] += rbuf[n]

    second_pass([s_ho, s_o, s_lq])
    add_mate(s_ho)
    bsend(0, s_ho, dev(q, yy, c))
    second_pass([s_hq, s_hw])
    add_mate(s_o)
    bsend(1, s_o, dev(w, yy, c))
    add_mate(s_lq)
    bsend(2, s_lq, dev(x, yy + l, c))
    add_mate(s_hq)
    from_q, from_y = dev(q, yy, c), dev(x, yy + h, c)
    hq_to = (jnp.where(c == 0, from_q[0], from_y[0]), jnp.where(c == 0, from_q[1], from_y[1]))
    bsend(3, s_hq, hq_to)
    second_pass([s_q, s_w, s_hx, s_lx])
    add_mate(s_hw)
    badd(0, s_hw)
    bsend(4, s_hw, dev(x, yy + h, c))
    second_pass([own])
    add_mate(s_q)
    add_mate(s_w)
    add_mate(s_hx)
    add_mate(s_lx)
    add_mate(own)
    bsend(5, s_lx, dev(x, yy + l, c))
    badd(1, s_q)
    badd(2, s_q)
    badd(3, jnp.where(c == 0, s_hx, s_q))
    bsend(6, s_q, dev(q, yy, c))
    bsend(7, s_hx, dev(x, yy + h, c))
    badd(4, s_w)
    bsend(8, s_w, dev(w, yy, c))
    for n in (5, 6, 7, 8):
        back[n].wait_recv()
    fg_out[...] = (win[own] + rbuf[5] + rbuf[6] + rbuf[7] + rbuf[8]).T

    @pl.loop(1, PLANE)
    def _(d):
        ac_copy(d).wait_recv()

    for cp in back + [rs0, rs1, rs2, ag0, ag1, ag2]:
        cp.wait_send()
    for i in range(WIN // 2):
        mate_copy(2 * i + 1 - c).wait_send()

    @pl.loop(1, PLANE)
    def _(d):
        aa_copy(d).wait_send()
        ac_copy(d).wait_send()

    @pl.loop(1, nz)
    def _(d):
        ab_copy(d).wait_send()


def shards(features, weight, cotangent, tile_row, tile_col, tile_count, tile_values):
    tile_rows = tile_row[0, 0]
    tile_cols = tile_col[0, 0]
    slot_ids = jnp.arange(SLOTS, dtype=jnp.int32)
    live = slot_ids < tile_count[0, 0]
    row_index = lax.axis_index("row")
    total_tiles = TPB * lax.axis_size("row")
    position = jnp.mod(tile_cols - (row_index - SPAN) * TPB, total_tiles)
    places = TPB * BAND_TILES
    key = jnp.where(live, tile_rows * BAND_TILES + position, places + slot_ids)
    before = (key[None, :] < key[:, None]) | ((key[None, :] == key[:, None]) & (slot_ids[None, :] < slot_ids[:, None]))
    rank = jnp.sum(before.astype(jnp.int32), axis=1)
    hit = rank[None, :] == slot_ids[:, None]
    perm = jnp.sum(jnp.where(hit, slot_ids[None, :], 0), axis=1)
    first = ~jnp.any((key[None, :] == key[:, None]) & (slot_ids[None, :] < slot_ids[:, None]), axis=1)
    keep = jnp.sum(jnp.where(hit & ~first[None, :], 1.0, 0.0), axis=1)
    spots = jnp.arange(places, dtype=jnp.int32)
    upto = jnp.sum((key[None, :] <= spots[:, None]).astype(jnp.int32), axis=1)
    there = jnp.any(key[None, :] == spots[:, None], axis=1)
    place = jnp.where(there, upto - 1, SLOTS)

    nz = lax.axis_size("row") // 8
    smem = pl.BlockSpec(memory_space=pltpu.SMEM)
    vmem = pl.BlockSpec(memory_space=pltpu.VMEM)
    anywhere = pl.BlockSpec(memory_space=pl.ANY)
    sem = pltpu.SemaphoreType.DMA
    act, fg, wg = pl.pallas_call(
        kernel,
        out_shape=(
            jax.ShapeDtypeStruct((ROWS, F), F32),
            jax.ShapeDtypeStruct((ROWS, F), F32),
            jax.ShapeDtypeStruct((PLANE, F // PLANE, F), F32),
        ),
        in_specs=[anywhere, anywhere, anywhere, anywhere, smem, smem, smem],
        out_specs=(vmem, vmem, vmem),
        scratch_shapes=[
            pltpu.VMEM((SLOTS, TILE, TILE), F32),
            pltpu.VMEM((SLOTS + 1, TILE, TILE), F32),
            pltpu.VMEM((WIN, TPB * TILE, 2 * TILE), BF16),
            pltpu.VMEM((WIN, TPB * TILE, 2 * TILE), BF16),
            pltpu.VMEM((WIN, ROWS, F), F32),
            pltpu.VMEM((4 * ROWS, F), F32),
            pltpu.VMEM((2, ROWS, F), F32),
            pltpu.VMEM((ROWS, F), F32),
            pltpu.VMEM((ROWS, F), F32),
            pltpu.VMEM((4, F, ROWS), F32),
            pltpu.VMEM((2, F, 2 * ROWS), BF16),
            pltpu.VMEM((2, F, 2 * ROWS), BF16),
            pltpu.VMEM((WIN // 2, F, ROWS), F32),
            pltpu.VMEM((9, F, ROWS), F32),
            pltpu.VMEM((PLANE, F // PLANE, F), F32),
            pltpu.VMEM((PLANE, F // PLANE, F), F32),
            pltpu.VMEM((nz, F // PLANE, F), F32),
            pltpu.VMEM((F // PLANE, F), F32),
            pltpu.VMEM((ROWS, F), F32),
            pltpu.VMEM((F, F), F32),
            sem((4,)), sem((19,)), sem((WIN,)), sem((1,)), sem((1,)), sem((3,)), sem((3,)), sem((3,)), sem((4,)),
            sem((WIN // 2,)), sem((WIN // 2,)), sem((9,)), sem((9,)),
            sem((PLANE,)), sem((PLANE,)), sem((nz,)), sem((nz,)), sem((PLANE,)), sem((PLANE,)),
        ],
        compiler_params=pltpu.CompilerParams(
            collective_id=0, has_side_effects=True, vmem_limit_bytes=62 * 1024 * 1024
        ),
    )(features, weight, cotangent, tile_values[0, 0], perm, keep, place)
    return act, fg, wg.reshape(F, F)


def solution(mesh):
    placed = (
        P(("row", "rep"), None),
        P(),
        P(("row", "rep"), None),
        P("row", "rep", None),
        P("row", "rep", None),
        P("row", "rep"),
        P("row", "rep", None, None, None),
    )
    return jax.shard_map(
        shards,
        mesh=mesh,
        in_specs=placed,
        out_specs=(P(("row", "rep"), None), P(("row", "rep"), None), P()),
        check_vma=False,
    )
```

```python
import jax
import jax.numpy as jnp
from jax import lax
from jax.experimental import pallas as pl
from jax.experimental.pallas import tpu as pltpu
from jax.sharding import PartitionSpec as P

TILE = 128
TPB = 8
SPAN = 2
SLOTS = 128
F = 256
ROWS = 256
WIN = 20
BAND_TILES = 40
PLANE = 32
PARTS_F = 2
PARTS_B = 4
HALF = 128
MESH = pl.DeviceIdType.MESH
F32 = jnp.float32
BF16 = jnp.bfloat16


def split(value):
    high = value.astype(BF16)
    low = (value - high.astype(F32)).astype(BF16)
    return high, low


def dot(a, b):
    return jnp.dot(a, b, preferred_element_type=F32)


def dot_t(a, b):
    return lax.dot_general(a, b, (((1,), (1,)), ((), ())), preferred_element_type=F32)


def dot3(op, a, b):
    ah, al = split(a)
    bh, bl = split(b)
    return op(ah, bh) + (op(al, bh) + op(ah, bl))


def choose(i, values):
    out = values[0]
    for k in range(1, len(values)):
        out = jnp.where(i == k, values[k], out)
    return out


def plan_tiles(row, total_tiles, rows, cols, count, plan):
    sub = lax.broadcasted_iota(jnp.int32, (SLOTS, SLOTS), 0)
    lane = lax.broadcasted_iota(jnp.int32, (SLOTS, SLOTS), 1)
    line = lax.broadcasted_iota(jnp.int32, (1, SLOTS), 1)

    def total(mask_or_value):
        return jnp.sum(mask_or_value, axis=0, keepdims=True)

    def ones(mask):
        return jnp.where(mask, 1, 0)

    position = cols - (row - SPAN) * TPB
    position = jnp.where(position < 0, position + total_tiles, position)
    position = jnp.where(position >= total_tiles, position - total_tiles, position)
    key = jnp.where(line < count, rows * BAND_TILES + position, TPB * BAND_TILES + line)
    key_r = jnp.broadcast_to(key, (SLOTS, SLOTS))
    key_c = key_r.T
    twin = ones((key_c == key_r) & (sub < lane))
    rank = total(ones(key_c < key_r) + twin)
    again = jnp.minimum(total(twin), 1)
    code = jnp.broadcast_to(rank * 2 + again, (SLOTS, SLOTS)).T
    again_c = code & 1
    hit = code - again_c == lane * 2
    plan[0:1, :] = total(jnp.where(hit, sub, 0))
    plan[1:2, :] = total(jnp.where(hit, again_c, 0))
    for part in range(3):
        spot = lane + part * SLOTS
        upto = total(ones(key_c <= spot))
        there = total(ones(key_c == spot))
        plan[2 + part:3 + part, :] = jnp.where(there > 0, upto - 1, SLOTS)


def deliver(act, fg, wg, act_out, fg_out, wg_out, stage, sem_in, sem_out):
    pairs = ((act, act_out), (fg, fg_out), (wg, wg_out))
    inward = [pltpu.make_async_copy(src, stage.at[i], sem_in.at[i]) for i, (src, _) in enumerate(pairs)]
    outward = [pltpu.make_async_copy(stage.at[i], dst, sem_out.at[i]) for i, (_, dst) in enumerate(pairs)]
    for cp in inward:
        cp.start()
    for cp, onward in zip(inward, outward):
        cp.wait()
        onward.start()
    for cp in outward:
        cp.wait()


def kernel(
    feat, weight, cot, tiles, tile_row, tile_col, tile_count,
    act_out, fg_out, wg_out,
    tilebuf, run, dense_h, dense_l, win, acc, rs_in, rs_mid, rs_send, gt, gt_h, gt_l, mrecv, rbuf,
    wg_loc, ar_a, ar_b, wg_sum, wg_all, cot_v, w_v, row_v, col_v, count_v, plan_v, plan,
    loc_sem, fs_sem, fr_sem, rs_s, rs_r, ag_s, ag_r, bm_s, bm_r, br_s, br_r,
    aa_s, aa_r, ab_s, ab_r, ac_s, ac_r,
):
    row = lax.axis_index("row")
    rep = lax.axis_index("rep")
    yy = lax.div(row, 2)
    xl = lax.div(rep, 2)
    c = lax.rem(rep, 2)
    xh = lax.rem(row, 2)
    x = xh * 2 + xl
    q = x + 1 - 2 * xl
    w = 3 - x
    o = lax.rem(x + 2, 4)
    h = 2 * xh - 1
    l = 1 - 2 * xh
    nyy = lax.axis_size("row") // 2

    def dev(xx, yv, cc):
        yv = lax.rem(yv + nyy, nyy)
        return (yv * 2 + lax.div(xx, 2), lax.rem(xx, 2) * 2 + cc)

    def slot(at, dyy, xx, cc):
        return (2 * dyy + lax.div(xx, 2) - lax.div(at, 2) + SPAN) * 4 + lax.rem(xx, 2) * 2 + cc

    mate = dev(x, yy, 1 - c)
    zi = lax.div(row, 8)
    nz = nyy // 4
    m_me = lax.rem(row, 8) * 4 + rep

    def plane_dev(m):
        return (zi * 8 + lax.div(m, 4), lax.rem(m, 4))

    def remote(src, dst, ssem, rsem, to):
        return pltpu.make_async_remote_copy(
            src_ref=src, dst_ref=dst, send_sem=ssem, recv_sem=rsem, device_id=to, device_id_type=MESH
        )

    tile_cp = pltpu.make_async_copy(tiles, tilebuf, loc_sem.at[0])
    tile_cp.start()
    own = slot(x, 0, x, c)
    feat_cp = pltpu.make_async_copy(feat, win.at[own], loc_sem.at[1])
    feat_cp.start()
    cot_cp = pltpu.make_async_copy(cot, cot_v, loc_sem.at[2])
    cot_cp.start()
    w_cp = pltpu.make_async_copy(weight, w_v, loc_sem.at[3])
    w_cp.start()
    list_cps = [
        pltpu.make_async_copy(src, dst, loc_sem.at[4 + i])
        for i, (src, dst) in enumerate(((tile_row, row_v), (tile_col, col_v), (tile_count, count_v)))
    ]
    for cp in list_cps:
        cp.start()

    bar = pltpu.get_barrier_semaphore()

    def greet(to):
        pl.semaphore_signal(bar, inc=1, device_id=to, device_id_type=MESH)

    @pl.loop(1, PLANE)
    def _(d):
        greet(plane_dev(lax.rem(m_me + d, PLANE)))

    @pl.loop(1, nz)
    def _(d):
        greet((lax.rem(row + 8 * d, nz * 8), rep))

    greet(dev(x, yy + 1, c))
    greet(dev(x, yy - 1, c))
    pl.semaphore_wait(bar, PLANE - 1 + nz - 1 + 2)

    sends = []

    def piece(k, parts):
        return pl.ds(k * (ROWS // parts), ROWS // parts)

    def fsend(n, k, src, dst_slot, to):
        part = piece(k, PARTS_F)
        cp = remote(src.at[part], win.at[dst_slot, part], fs_sem.at[n, k], fr_sem.at[dst_slot, k], to)
        cp.start()
        sends.append(cp)

    def frecv(s, k):
        part = piece(k, PARTS_F)
        remote(feat.at[part], win.at[s, part], fs_sem.at[0, k], fr_sem.at[s, k], mate).wait_recv()

    for k in range(PARTS_F):
        fsend(1, k, feat, slot(x, -1, x, c), dev(x, yy + 1, c))
        fsend(2, k, feat, slot(x, 1, x, c), dev(x, yy - 1, c))
        fsend(0, k, feat, slot(q, 0, x, c), dev(q, yy, c))
        fsend(3, k, feat, slot(w, 0, x, c), dev(w, yy, c))
    for k in range(PARTS_F):
        fsend(4, k, feat, own, mate)

    acc[...] = jnp.zeros_like(acc)
    run[SLOTS] = jnp.zeros((TILE, TILE), F32)
    for cp in list_cps:
        cp.wait()
    plan_tiles(row, nyy * 2 * TPB, row_v[0], col_v[0], count_v[...], plan_v)
    plan_cp = pltpu.make_async_copy(plan_v, plan, loc_sem.at[7])
    plan_cp.start()
    plan_cp.wait()
    tile_cp.wait()

    def merge(t, prev):
        value = prev * plan[1, t].astype(F32) + tilebuf[plan[0, t]]
        run[t] = value
        return value

    lax.fori_loop(0, SLOTS, merge, jnp.zeros((TILE, TILE), F32))

    feat_cp.wait()

    def forward(s):
        for r in range(TPB):
            for half in range(2):
                spot = s * 2 + (r * BAND_TILES + half)
                high, low = split(run[plan[2 + lax.div(spot, SLOTS), lax.rem(spot, SLOTS)]])
                dense_h[s, r * TILE:(r + 1) * TILE, half * TILE:(half + 1) * TILE] = high
                dense_l[s, r * TILE:(r + 1) * TILE, half * TILE:(half + 1) * TILE] = low
        xh_, xl_ = split(win[s])
        a = dense_h[s]
        acc[...] += dot(a, xh_) + (dot(dense_l[s], xh_) + dot(a, xl_))

    def forward_group(slots):
        @pl.loop(0, len(slots))
        def _(i):
            forward(choose(i, slots))

    def forward_recv_group(slots):
        @pl.loop(0, len(slots))
        def _(i):
            s = choose(i, slots)
            for k in range(PARTS_F):
                frecv(s, k)
            forward(s)

    def flip(s):
        return s + 1 - 2 * c

    s_q, s_w = slot(x, 0, q, c), slot(x, 0, w, c)
    s_hx, s_lx = slot(x, h, x, c), slot(x, l, x, c)
    s_o, s_hw = slot(x, 0, o, c), slot(x, h, w, c)
    s_lq, s_hq = slot(x, l, q, c), slot(x, h, q, c)
    s_ho = slot(x, h, o, c)

    qh_src = jnp.where(c == 0, s_hx, s_q)
    qh_dst = jnp.where(c == 0, slot(q, h, x, c), slot(x, h, q, c))
    to_q, to_y = dev(q, yy, c), dev(x, yy - h, c)
    qh_to = (jnp.where(c == 0, to_q[0], to_y[0]), jnp.where(c == 0, to_q[1], to_y[1]))

    def relay(n, k, s):
        frecv(s, k)
        fsend(n, k, win.at[s], s, mate)

    forward_group([own])
    for k in range(PARTS_F):
        frecv(s_w, k)
        fsend(7, k, win.at[s_w], slot(x, h, w, c), dev(x, yy - h, c))
        frecv(s_q, k)
        fsend(6, k, win.at[s_q], slot(x, l, q, c), dev(x, yy + h, c))
        fsend(5, k, win.at[s_q], slot(w, 0, q, c), dev(w, yy, c))
        frecv(s_hx, k)
        fsend(8, k, win.at[qh_src], qh_dst, qh_to)
        fsend(9, k, win.at[s_q], s_q, mate)
        fsend(10, k, win.at[s_w], s_w, mate)
        fsend(11, k, win.at[s_hx], s_hx, mate)
        relay(12, k, s_lx)
        if k == 0:
            forward_recv_group([flip(own)])
    forward_group([s_q, s_w, s_hx, s_lx])

    for k in range(PARTS_F):
        frecv(s_hw, k)
        fsend(13, k, win.at[s_hw], slot(q, h, w, c), dev(q, yy, c))
        fsend(14, k, win.at[s_hw], s_hw, mate)
        if k == 0:
            forward_recv_group([flip(s_q), flip(s_w)])
    forward_recv_group([flip(s_hx), flip(s_lx)])
    for k in range(PARTS_F):
        relay(15, k, s_o)
        relay(16, k, s_lq)
    forward_group([s_hw, s_o, s_lq])
    for k in range(PARTS_F):
        relay(17, k, s_hq)
    forward_group([s_hq])
    forward_recv_group([flip(s_hw), flip(s_o)])
    relay(18, 0, s_ho)
    forward_recv_group([flip(s_lq)])
    for k in range(1, PARTS_F):
        relay(18, k, s_ho)
    forward_recv_group([flip(s_hq)])
    forward_group([s_ho])
    forward_recv_group([flip(s_ho)])

    k_o = (1 - xl) * 2 + c
    k_m = xl * 2 + 1 - c
    k_mo = (1 - xl) * 2 + 1 - c

    def chunk(k):
        return acc.at[pl.ds(pl.multiple_of(k * ROWS, ROWS), ROWS)]

    def half_of(k, n):
        return acc.at[pl.ds(pl.multiple_of(k * ROWS + n * HALF, HALF), HALF)]

    halves = [pl.ds(n * HALF, HALF) for n in range(2)]
    rs0 = [remote(half_of(k_mo, n), rs_in.at[0, halves[n]], rs_s.at[n], rs_r.at[n], mate) for n in range(2)]
    rs1 = [remote(half_of(k_m, n), rs_in.at[1, halves[n]], rs_s.at[2 + n], rs_r.at[2 + n], mate) for n in range(2)]
    rs2 = [remote(rs_send.at[halves[n]], rs_mid.at[halves[n]], rs_s.at[4 + n], rs_r.at[4 + n], dev(q, yy, c)) for n in range(2)]
    for cp in rs0 + rs1:
        cp.start()
    for cp in sends:
        cp.wait_send()
    for n in range(2):
        rs0[n].wait_recv()
        rs_send[halves[n]] = half_of(k_o, n)[...] + rs_in[0, halves[n]]
        rs2[n].start()
    cot_cp.wait()
    w_cp.wait()
    wh, wl = split(w_v[...])

    def gt_copy(k, n, number, to):
        return remote(gt.at[k, n], gt.at[k, n], ag_s.at[number, n], ag_r.at[k, n], to)

    def grecv(k, n):
        gt_copy(k, n, 0, mate).wait_recv()

    ag = []
    aggs, gps = [], []
    for n in range(2):
        rs1[n].wait_recv()
        part = half_of(rep, n)[...] + rs_in[1, halves[n]]
        rs2[n].wait_recv()
        agg = part + rs_mid[halves[n]]
        ah, al = split(agg)
        pre = dot(ah, wh) + (dot(al, wh) + dot(ah, wl))
        sig = jax.nn.sigmoid(pre)
        gp = cot_v[halves[n]] * (sig * (1.0 + pre * (1.0 - sig)))
        ph, plow = split(gp)
        gt[rep, n] = dot_t(wh, ph) + (dot_t(wl, ph) + dot_t(wh, plow))
        for number, to in ((0, dev(q, yy, c)), (1, mate)):
            cp = gt_copy(rep, n, number, to)
            cp.start()
            ag.append(cp)
        rs_in[0, halves[n]] = pre * sig
        aggs.append(agg)
        gps.append(gp)
    act_cp = pltpu.make_async_copy(rs_in.at[0], act_out, loc_sem.at[8])
    act_cp.start()
    agg = jnp.concatenate(aggs, axis=0)
    gp = jnp.concatenate(gps, axis=0)
    wg = dot3(dot, agg.T, gp).reshape(PLANE, F // PLANE, F)
    wg_loc[...] = wg

    def ar_copy(d, src, dst, ssem, rsem):
        return remote(src, dst, ssem.at[d], rsem.at[d], plane_dev(lax.rem(m_me + d, PLANE)))

    def aa_copy(d):
        return ar_copy(d, wg_loc.at[lax.rem(m_me + d, PLANE)], ar_a.at[m_me], aa_s, aa_r)

    def ab_copy(d):
        return remote(wg_sum, ar_b.at[zi], ab_s.at[d], ab_r.at[d], (lax.rem(row + 8 * d, nz * 8), rep))

    def ac_copy(d):
        return ar_copy(d, wg_all.at[m_me], wg_all.at[m_me], ac_s, ac_r)

    @pl.loop(1, PLANE)
    def _(d):
        aa_copy(d).start()

    ar_a[m_me] = wg_loc[m_me]

    for n in range(2):
        grecv(k_m, n)

    def spread(pair):
        for core in range(2):
            for n in range(2):
                high, low = split(gt[pair * 2 + core, n])
                start = core * ROWS + n * HALF
                gt_h[pair, :, start:start + HALF] = high
                gt_l[pair, :, start:start + HALF] = low

    def backward(s, pair):
        rows = pl.ds(pl.multiple_of(pair * 2 * ROWS, 2 * ROWS), 2 * ROWS)
        a = dense_h[s, rows, :]
        g = gt_h[pair]
        return dot(g, a) + (dot(gt_l[pair], a) + dot(g, dense_l[s, rows, :]))

    spread(xl)

    def first_pass(slots):
        @pl.loop(0, len(slots))
        def _(i):
            s = choose(i, slots)
            win[s] = backward(s, xl)

    early = [s_ho, s_hw, s_o, s_lq, s_hq, s_q]
    early = [v for s in early for v in (flip(s), s)]
    first_pass(early[:4])
    for n in range(2):
        grecv(k_o, n)
        cp = gt_copy(k_o, n, 2, mate)
        cp.start()
        ag.append(cp)
        if n == 0:
            first_pass(early[4:10])
    first_pass(early[10:])
    for n in range(2):
        grecv(k_mo, n)
    spread(1 - xl)

    def mate_copy(s):
        i = lax.div(s, 2)
        return remote(win.at[s], mrecv.at[i], bm_s.at[i], bm_r.at[i], mate)

    def second_pass(s, whole=False):
        @pl.loop(0, 2)
        def _(i):
            at = jnp.where(i == 0, flip(s), s)
            if whole:
                win[at] = backward(at, xl) + backward(at, 1 - xl)
            else:
                win[at] += backward(at, 1 - xl)

            @pl.when(i == 0)
            def _():
                mate_copy(at).start()

    def add_mate(s):
        mate_copy(s).wait_recv()
        win[s] += mrecv[lax.div(s, 2)]

    back = {}

    def bsend(n, k, s, to):
        part = piece(k, PARTS_B)
        cp = remote(win.at[s, part], rbuf.at[n, part], br_s.at[n, k], br_r.at[n, k], to)
        cp.start()
        back[n, k] = cp

    def bsend_all(n, s, to):
        for k in range(PARTS_B):
            bsend(n, k, s, to)

    def badd(n, k, s):
        part = piece(k, PARTS_B)
        back[n, k].wait_recv()
        win[s, part] += rbuf[n, part]

    from_q, from_y = dev(q, yy, c), dev(x, yy + h, c)
    hq_to = (jnp.where(c == 0, from_q[0], from_y[0]), jnp.where(c == 0, from_q[1], from_y[1]))
    second_pass(s_ho)
    second_pass(s_hw)
    add_mate(s_ho)
    bsend_all(0, s_ho, dev(q, yy, c))
    second_pass(s_o)
    add_mate(s_hw)
    second_pass(s_lq)
    add_mate(s_o)
    bsend_all(1, s_o, dev(w, yy, c))
    second_pass(s_hq)
    add_mate(s_lq)
    bsend_all(2, s_lq, dev(x, yy + l, c))
    second_pass(s_q)
    add_mate(s_hq)
    bsend_all(3, s_hq, hq_to)

    def pass_on_hw(k):
        badd(0, k, s_hw)
        bsend(4, k, s_hw, dev(x, yy + h, c))

    pass_on_hw(0)
    second_pass(s_lx, whole=True)
    pass_on_hw(1)
    add_mate(s_q)
    second_pass(s_hx, whole=True)
    for k in range(2, PARTS_B):
        pass_on_hw(k)
    add_mate(s_lx)
    bsend_all(5, s_lx, dev(x, yy + l, c))
    second_pass(s_w, whole=True)
    @pl.loop(1, PLANE)
    def _(d):
        aa_copy(d).wait_recv()

    total = ar_a[0]
    for k in range(1, PLANE):
        total = total + ar_a[k]
    wg_sum[...] = total
    ar_b[zi] = total

    @pl.loop(1, nz)
    def _(d):
        ab_copy(d).start()

    add_mate(s_hx)
    s_3 = jnp.where(c == 0, s_hx, s_q)

    def pass_on_q(k):
        badd(1, k, s_q)
        badd(2, k, s_q)
        badd(3, k, s_3)
        bsend(6, k, s_q, dev(q, yy, c))
        bsend(7, k, s_hx, dev(x, yy + h, c))

    def pass_on_w(k):
        badd(4, k, s_w)
        bsend(8, k, s_w, dev(w, yy, c))

    pass_on_q(0)
    second_pass(own, whole=True)
    add_mate(s_w)
    pass_on_w(0)
    for k in range(1, PARTS_B):
        pass_on_q(k)
        pass_on_w(k)
    add_mate(own)
    @pl.loop(1, nz)
    def _(d):
        ab_copy(d).wait_recv()

    total = ar_b[0]
    for k in range(1, nz):
        total = total + ar_b[k]
    wg_all[m_me] = total

    @pl.loop(1, PLANE)
    def _(d):
        ac_copy(d).start()

    for k in range(PARTS_B):
        for n in (5, 6, 7, 8):
            badd(n, k, own)
    rs_in[1] = win[own].T
    fg_cp = pltpu.make_async_copy(rs_in.at[1], fg_out, loc_sem.at[9])
    fg_cp.start()

    @pl.loop(1, PLANE)
    def _(d):
        ac_copy(d).wait_recv()

    wg_cp = pltpu.make_async_copy(wg_all, wg_out, loc_sem.at[10])
    wg_cp.start()
    for cp in list(back.values()) + rs0 + rs1 + rs2 + ag:
        cp.wait_send()
    for i in range(WIN // 2):
        mate_copy(2 * i + 1 - c).wait_send()

    @pl.loop(1, PLANE)
    def _(d):
        aa_copy(d).wait_send()
        ac_copy(d).wait_send()

    @pl.loop(1, nz)
    def _(d):
        ab_copy(d).wait_send()

    act_cp.wait()
    fg_cp.wait()
    wg_cp.wait()


def shards(features, weight, cotangent, tile_row, tile_col, tile_count, tile_values):
    nz = lax.axis_size("row") // 8
    anywhere = pl.BlockSpec(memory_space=pl.ANY)
    sem = pltpu.SemaphoreType.DMA
    act, fg, wg = pl.pallas_call(
        kernel,
        out_shape=(
            jax.ShapeDtypeStruct((ROWS, F), F32),
            jax.ShapeDtypeStruct((ROWS, F), F32),
            jax.ShapeDtypeStruct((PLANE, F // PLANE, F), F32),
        ),
        in_specs=[anywhere] * 7,
        out_specs=(anywhere,) * 3,
        scratch_shapes=[
            pltpu.VMEM((SLOTS, TILE, TILE), F32),
            pltpu.VMEM((SLOTS + 1, TILE, TILE), F32),
            pltpu.VMEM((WIN, TPB * TILE, 2 * TILE), BF16),
            pltpu.VMEM((WIN, TPB * TILE, 2 * TILE), BF16),
            pltpu.VMEM((WIN, ROWS, F), F32),
            pltpu.VMEM((4 * ROWS, F), F32),
            pltpu.VMEM((2, ROWS, F), F32),
            pltpu.VMEM((ROWS, F), F32),
            pltpu.VMEM((ROWS, F), F32),
            pltpu.VMEM((4, 2, F, HALF), F32),
            pltpu.VMEM((2, F, 2 * ROWS), BF16),
            pltpu.VMEM((2, F, 2 * ROWS), BF16),
            pltpu.VMEM((WIN // 2, F, ROWS), F32),
            pltpu.VMEM((9, F, ROWS), F32),
            pltpu.VMEM((PLANE, F // PLANE, F), F32),
            pltpu.VMEM((PLANE, F // PLANE, F), F32),
            pltpu.VMEM((nz, F // PLANE, F), F32),
            pltpu.VMEM((F // PLANE, F), F32),
            pltpu.VMEM((PLANE, F // PLANE, F), F32),
            pltpu.VMEM((ROWS, F), F32),
            pltpu.VMEM((F, F), F32),
            pltpu.VMEM((1, 1, SLOTS), jnp.int32),
            pltpu.VMEM((1, 1, SLOTS), jnp.int32),
            pltpu.VMEM((1, 1), jnp.int32),
            pltpu.VMEM((8, SLOTS), jnp.int32),
            pltpu.SMEM((8, SLOTS), jnp.int32),
            sem((11,)), sem((19, PARTS_F)), sem((WIN, PARTS_F)), sem((6,)), sem((6,)), sem((3, 2)), sem((4, 2)),
            sem((WIN // 2,)), sem((WIN // 2,)), sem((9, PARTS_B)), sem((9, PARTS_B)),
            sem((PLANE,)), sem((PLANE,)), sem((nz,)), sem((nz,)), sem((PLANE,)), sem((PLANE,)),
        ],
        compiler_params=pltpu.CompilerParams(
            collective_id=0, has_side_effects=True, vmem_limit_bytes=62 * 1024 * 1024
        ),
    )(features, weight, cotangent, tile_values[0, 0], tile_row, tile_col, tile_count)
    shape = jax.ShapeDtypeStruct((ROWS, F), F32)
    return pl.pallas_call(
        deliver,
        out_shape=(shape,) * 3,
        in_specs=[anywhere] * 3,
        out_specs=(anywhere,) * 3,
        scratch_shapes=[pltpu.VMEM((3, ROWS, F), F32), sem((3,)), sem((3,))],
    )(act, fg, wg.reshape(F, F))


def solution(mesh):
    placed = (
        P(("row", "rep"), None),
        P(),
        P(("row", "rep"), None),
        P("row", "rep", None),
        P("row", "rep", None),
        P("row", "rep"),
        P("row", "rep", None, None, None),
    )
    return jax.shard_map(
        shards,
        mesh=mesh,
        in_specs=placed,
        out_specs=(P(("row", "rep"), None), P(("row", "rep"), None), P()),
        check_vma=False,
    )
```

```python
import jax
import jax.numpy as jnp
from jax import lax
from jax.experimental import pallas as pl
from jax.experimental.pallas import tpu as pltpu
from jax.sharding import PartitionSpec as P

TILE = 128
TPB = 8
SPAN = 2
SLOTS = 128
F = 256
ROWS = 256
WIN = 20
BAND_TILES = 40
PLANE = 32
PARTS_F = 2
PARTS_B = 4
HALF = 128
MESH = pl.DeviceIdType.MESH
F32 = jnp.float32
BF16 = jnp.bfloat16


def split(value):
    high = value.astype(BF16)
    low = (value - high.astype(F32)).astype(BF16)
    return high, low


def dot(a, b):
    return jnp.dot(a, b, preferred_element_type=F32)


def dot_t(a, b):
    return lax.dot_general(a, b, (((1,), (1,)), ((), ())), preferred_element_type=F32)


def dot3(op, a, b):
    ah, al = split(a)
    bh, bl = split(b)
    return op(ah, bh) + (op(al, bh) + op(ah, bl))


def choose(i, values):
    out = values[0]
    for k in range(1, len(values)):
        out = jnp.where(i == k, values[k], out)
    return out


def plan_tiles(row, total_tiles, rows, cols, count, plan):
    sub = lax.broadcasted_iota(jnp.int32, (SLOTS, SLOTS), 0)
    lane = lax.broadcasted_iota(jnp.int32, (SLOTS, SLOTS), 1)
    line = lax.broadcasted_iota(jnp.int32, (1, SLOTS), 1)

    def total(mask_or_value):
        return jnp.sum(mask_or_value, axis=0, keepdims=True)

    def ones(mask):
        return jnp.where(mask, 1, 0)

    position = cols - (row - SPAN) * TPB
    position = jnp.where(position < 0, position + total_tiles, position)
    position = jnp.where(position >= total_tiles, position - total_tiles, position)
    key = jnp.where(line < count, rows * BAND_TILES + position, TPB * BAND_TILES + line)
    key_r = jnp.broadcast_to(key, (SLOTS, SLOTS))
    key_c = key_r.T
    twin = ones((key_c == key_r) & (sub < lane))
    rank = total(ones(key_c < key_r) + twin)
    again = jnp.minimum(total(twin), 1)
    code = jnp.broadcast_to(rank * 2 + again, (SLOTS, SLOTS)).T
    again_c = code & 1
    hit = code - again_c == lane * 2
    plan[0:1, :] = total(jnp.where(hit, sub, 0))
    plan[1:2, :] = total(jnp.where(hit, again_c, 0))
    for part in range(3):
        spot = lane + part * SLOTS
        upto = total(ones(key_c <= spot))
        there = total(ones(key_c == spot))
        plan[2 + part:3 + part, :] = jnp.where(there > 0, upto - 1, SLOTS)


def kernel(
    feat, weight, cot, tiles, tile_row, tile_col, tile_count,
    act_out, fg_out, wg_out,
    tilebuf, run, dense_h, dense_l, win, acc, rs_in, rs_mid, rs_send, gt, gt_h, gt_l, mrecv, rbuf,
    wg_loc, ar_a, ar_b, wg_sum, wg_all, cot_v, w_v, row_v, col_v, count_v, plan_v, plan,
    loc_sem, fs_sem, fr_sem, rs_s, rs_r, ag_s, ag_r, bm_s, bm_r, br_s, br_r,
    aa_s, aa_r, ab_s, ab_r, ac_s, ac_r,
):
    row = lax.axis_index("row")
    rep = lax.axis_index("rep")
    yy = lax.div(row, 2)
    xl = lax.div(rep, 2)
    c = lax.rem(rep, 2)
    xh = lax.rem(row, 2)
    x = xh * 2 + xl
    q = x + 1 - 2 * xl
    w = 3 - x
    o = lax.rem(x + 2, 4)
    h = 2 * xh - 1
    l = 1 - 2 * xh
    nyy = lax.axis_size("row") // 2

    def dev(xx, yv, cc):
        yv = lax.rem(yv + nyy, nyy)
        return (yv * 2 + lax.div(xx, 2), lax.rem(xx, 2) * 2 + cc)

    def slot(at, dyy, xx, cc):
        return (2 * dyy + lax.div(xx, 2) - lax.div(at, 2) + SPAN) * 4 + lax.rem(xx, 2) * 2 + cc

    mate = dev(x, yy, 1 - c)
    zi = lax.div(row, 8)
    nz = nyy // 4
    m_me = lax.rem(row, 8) * 4 + rep

    def plane_dev(m):
        return (zi * 8 + lax.div(m, 4), lax.rem(m, 4))

    def remote(src, dst, ssem, rsem, to):
        return pltpu.make_async_remote_copy(
            src_ref=src, dst_ref=dst, send_sem=ssem, recv_sem=rsem, device_id=to, device_id_type=MESH
        )

    tile_cp = pltpu.make_async_copy(tiles, tilebuf, loc_sem.at[0])
    tile_cp.start()
    own = slot(x, 0, x, c)
    feat_cp = pltpu.make_async_copy(feat, win.at[own], loc_sem.at[1])
    feat_cp.start()
    cot_cp = pltpu.make_async_copy(cot, cot_v, loc_sem.at[2])
    cot_cp.start()
    w_cp = pltpu.make_async_copy(weight, w_v, loc_sem.at[3])
    w_cp.start()
    list_cps = [
        pltpu.make_async_copy(src, dst, loc_sem.at[4 + i])
        for i, (src, dst) in enumerate(((tile_row, row_v), (tile_col, col_v), (tile_count, count_v)))
    ]
    for cp in list_cps:
        cp.start()

    bar = pltpu.get_barrier_semaphore()

    def greet(to):
        pl.semaphore_signal(bar, inc=1, device_id=to, device_id_type=MESH)

    @pl.loop(1, PLANE)
    def _(d):
        greet(plane_dev(lax.rem(m_me + d, PLANE)))

    @pl.loop(1, nz)
    def _(d):
        greet((lax.rem(row + 8 * d, nz * 8), rep))

    greet(dev(x, yy + 1, c))
    greet(dev(x, yy - 1, c))
    pl.semaphore_wait(bar, PLANE - 1 + nz - 1 + 2)

    sends = []

    def piece(k, parts):
        return pl.ds(k * (ROWS // parts), ROWS // parts)

    def fsend(n, k, src, dst_slot, to):
        part = piece(k, PARTS_F)
        cp = remote(src.at[part], win.at[dst_slot, part], fs_sem.at[n, k], fr_sem.at[dst_slot, k], to)
        cp.start()
        sends.append(cp)

    def frecv(s, k):
        part = piece(k, PARTS_F)
        remote(feat.at[part], win.at[s, part], fs_sem.at[0, k], fr_sem.at[s, k], mate).wait_recv()

    for k in range(PARTS_F):
        fsend(1, k, feat, slot(x, -1, x, c), dev(x, yy + 1, c))
        fsend(2, k, feat, slot(x, 1, x, c), dev(x, yy - 1, c))
        fsend(0, k, feat, slot(q, 0, x, c), dev(q, yy, c))
        fsend(3, k, feat, slot(w, 0, x, c), dev(w, yy, c))
    for k in range(PARTS_F):
        fsend(4, k, feat, own, mate)

    acc[...] = jnp.zeros_like(acc)
    run[SLOTS] = jnp.zeros((TILE, TILE), F32)
    for cp in list_cps:
        cp.wait()
    plan_tiles(row, nyy * 2 * TPB, row_v[0], col_v[0], count_v[...], plan_v)
    plan_cp = pltpu.make_async_copy(plan_v, plan, loc_sem.at[7])
    plan_cp.start()
    plan_cp.wait()
    tile_cp.wait()

    def merge(t, prev):
        value = prev * plan[1, t].astype(F32) + tilebuf[plan[0, t]]
        run[t] = value
        return value

    lax.fori_loop(0, SLOTS, merge, jnp.zeros((TILE, TILE), F32))

    feat_cp.wait()

    def forward(s):
        for r in range(TPB):
            for half in range(2):
                spot = s * 2 + (r * BAND_TILES + half)
                high, low = split(run[plan[2 + lax.div(spot, SLOTS), lax.rem(spot, SLOTS)]])
                dense_h[s, r * TILE:(r + 1) * TILE, half * TILE:(half + 1) * TILE] = high
                dense_l[s, r * TILE:(r + 1) * TILE, half * TILE:(half + 1) * TILE] = low
        xh_, xl_ = split(win[s])
        a = dense_h[s]
        acc[...] += dot(a, xh_) + (dot(dense_l[s], xh_) + dot(a, xl_))

    def forward_group(slots):
        @pl.loop(0, len(slots))
        def _(i):
            forward(choose(i, slots))

    def forward_recv_group(slots):
        @pl.loop(0, len(slots))
        def _(i):
            s = choose(i, slots)
            for k in range(PARTS_F):
                frecv(s, k)
            forward(s)

    def flip(s):
        return s + 1 - 2 * c

    s_q, s_w = slot(x, 0, q, c), slot(x, 0, w, c)
    s_hx, s_lx = slot(x, h, x, c), slot(x, l, x, c)
    s_o, s_hw = slot(x, 0, o, c), slot(x, h, w, c)
    s_lq, s_hq = slot(x, l, q, c), slot(x, h, q, c)
    s_ho = slot(x, h, o, c)

    qh_src = jnp.where(c == 0, s_hx, s_q)
    qh_dst = jnp.where(c == 0, slot(q, h, x, c), slot(x, h, q, c))
    to_q, to_y = dev(q, yy, c), dev(x, yy - h, c)
    qh_to = (jnp.where(c == 0, to_q[0], to_y[0]), jnp.where(c == 0, to_q[1], to_y[1]))

    def relay(n, k, s):
        frecv(s, k)
        fsend(n, k, win.at[s], s, mate)

    forward_group([own])
    for k in range(PARTS_F):
        frecv(s_w, k)
        fsend(7, k, win.at[s_w], slot(x, h, w, c), dev(x, yy - h, c))
        frecv(s_q, k)
        fsend(6, k, win.at[s_q], slot(x, l, q, c), dev(x, yy + h, c))
        fsend(5, k, win.at[s_q], slot(w, 0, q, c), dev(w, yy, c))
        frecv(s_hx, k)
        fsend(8, k, win.at[qh_src], qh_dst, qh_to)
        fsend(9, k, win.at[s_q], s_q, mate)
        fsend(10, k, win.at[s_w], s_w, mate)
        fsend(11, k, win.at[s_hx], s_hx, mate)
        relay(12, k, s_lx)
        if k == 0:
            forward_recv_group([flip(own)])
    forward_group([s_q, s_w, s_hx, s_lx])

    for k in range(PARTS_F):
        frecv(s_hw, k)
        fsend(13, k, win.at[s_hw], slot(q, h, w, c), dev(q, yy, c))
        fsend(14, k, win.at[s_hw], s_hw, mate)
        if k == 0:
            forward_recv_group([flip(s_q), flip(s_w)])
    forward_recv_group([flip(s_hx), flip(s_lx)])
    for k in range(PARTS_F):
        relay(15, k, s_o)
        relay(16, k, s_lq)
    forward_group([s_hw, s_o, s_lq])
    for k in range(PARTS_F):
        relay(17, k, s_hq)
    relay(18, 0, s_ho)
    forward_group([s_hq])
    forward_recv_group([flip(s_hw), flip(s_o), flip(s_lq)])
    for k in range(1, PARTS_F):
        relay(18, k, s_ho)
    forward_recv_group([flip(s_hq)])
    forward_group([s_ho])
    forward_recv_group([flip(s_ho)])

    k_o = (1 - xl) * 2 + c
    k_m = xl * 2 + 1 - c
    k_mo = (1 - xl) * 2 + 1 - c

    def chunk(k):
        return acc.at[pl.ds(pl.multiple_of(k * ROWS, ROWS), ROWS)]

    def half_of(k, n):
        return acc.at[pl.ds(pl.multiple_of(k * ROWS + n * HALF, HALF), HALF)]

    halves = [pl.ds(n * HALF, HALF) for n in range(2)]
    rs0 = [remote(half_of(k_mo, n), rs_in.at[0, halves[n]], rs_s.at[n], rs_r.at[n], mate) for n in range(2)]
    rs1 = [remote(half_of(k_m, n), rs_in.at[1, halves[n]], rs_s.at[2 + n], rs_r.at[2 + n], mate) for n in range(2)]
    rs2 = [remote(rs_send.at[halves[n]], rs_mid.at[halves[n]], rs_s.at[4 + n], rs_r.at[4 + n], dev(q, yy, c)) for n in range(2)]
    for cp in rs0 + rs1:
        cp.start()
    for cp in sends:
        cp.wait_send()
    for n in range(2):
        rs0[n].wait_recv()
        rs_send[halves[n]] = half_of(k_o, n)[...] + rs_in[0, halves[n]]
        rs2[n].start()
    cot_cp.wait()
    w_cp.wait()
    wh, wl = split(w_v[...])

    def gt_copy(k, n, number, to):
        return remote(gt.at[k, n], gt.at[k, n], ag_s.at[number, n], ag_r.at[k, n], to)

    def grecv(k, n):
        gt_copy(k, n, 0, mate).wait_recv()

    ag = []
    aggs, gps = [], []
    for n in range(2):
        rs1[n].wait_recv()
        part = half_of(rep, n)[...] + rs_in[1, halves[n]]
        rs2[n].wait_recv()
        agg = part + rs_mid[halves[n]]
        ah, al = split(agg)
        pre = dot(ah, wh) + (dot(al, wh) + dot(ah, wl))
        sig = jax.nn.sigmoid(pre)
        gp = cot_v[halves[n]] * (sig * (1.0 + pre * (1.0 - sig)))
        ph, plow = split(gp)
        gt[rep, n] = dot_t(wh, ph) + (dot_t(wl, ph) + dot_t(wh, plow))
        for number, to in ((0, dev(q, yy, c)), (1, mate)):
            cp = gt_copy(rep, n, number, to)
            cp.start()
            ag.append(cp)
        rs_in[0, halves[n]] = pre * sig
        aggs.append(agg)
        gps.append(gp)
    act_cp = pltpu.make_async_copy(rs_in.at[0], act_out, loc_sem.at[8])
    act_cp.start()
    agg = jnp.concatenate(aggs, axis=0)
    gp = jnp.concatenate(gps, axis=0)
    wg = dot3(dot, agg.T, gp).reshape(PLANE, F // PLANE, F)
    wg_loc[...] = wg

    def ar_copy(d, src, dst, ssem, rsem):
        return remote(src, dst, ssem, rsem, plane_dev(lax.rem(m_me + d, PLANE)))

    def aa_copy(d):
        return ar_copy(d, wg_loc.at[lax.rem(m_me + d, PLANE)], ar_a.at[m_me], aa_s, aa_r)

    def ab_copy(d):
        return remote(wg_sum, ar_b.at[zi], ab_s, ab_r, (lax.rem(row + 8 * d, nz * 8), rep))

    def ac_copy(d):
        return ar_copy(d, wg_all.at[m_me], wg_all.at[m_me], ac_s, ac_r)

    ar_a[m_me] = wg_loc[m_me]

    for n in range(2):
        grecv(k_m, n)

    def spread(pair):
        for core in range(2):
            for n in range(2):
                high, low = split(gt[pair * 2 + core, n])
                start = core * ROWS + n * HALF
                gt_h[pair, :, start:start + HALF] = high
                gt_l[pair, :, start:start + HALF] = low

    def backward(s, pair):
        rows = pl.ds(pl.multiple_of(pair * 2 * ROWS, 2 * ROWS), 2 * ROWS)
        a = dense_h[s, rows, :]
        g = gt_h[pair]
        return dot(g, a) + (dot(gt_l[pair], a) + dot(g, dense_l[s, rows, :]))

    spread(xl)

    def first_pass(slots):
        @pl.loop(0, len(slots))
        def _(i):
            s = choose(i, slots)
            win[s] = backward(s, xl)

    early = [s_ho, s_hw, s_o, s_lq, s_hq, s_q]
    early = [v for s in early for v in (flip(s), s)]
    first_pass(early[:4])
    for n in range(2):
        grecv(k_o, n)
        cp = gt_copy(k_o, n, 2, mate)
        cp.start()
        ag.append(cp)
        if n == 0:
            first_pass(early[4:10])
    def aa_all():
        some = pl.ds(0, PLANE - 1)
        return remote(wg_loc.at[some], ar_a.at[some], aa_s, aa_r, mate)

    def ab_all():
        some = pl.ds(0, nz - 1)
        return remote(ar_b.at[some], ar_b.at[some], ab_s, ab_r, mate)

    def ac_all():
        some = pl.ds(0, PLANE - 1)
        return remote(wg_all.at[some], wg_all.at[some], ac_s, ac_r, mate)

    @pl.loop(1, PLANE)
    def _(d):
        aa_copy(d).start()

    first_pass(early[10:])
    for n in range(2):
        grecv(k_mo, n)
    spread(1 - xl)

    def mate_copy(s):
        i = lax.div(s, 2)
        return remote(win.at[s], mrecv.at[i], bm_s.at[i], bm_r.at[i], mate)

    def second_pass(s, whole=False):
        @pl.loop(0, 2)
        def _(i):
            at = jnp.where(i == 0, flip(s), s)
            if whole:
                win[at] = backward(at, xl) + backward(at, 1 - xl)
            else:
                win[at] += backward(at, 1 - xl)

            @pl.when(i == 0)
            def _():
                mate_copy(at).start()

    def add_mate(s):
        mate_copy(s).wait_recv()
        win[s] += mrecv[lax.div(s, 2)]

    back = {}

    def bsend(n, k, s, to):
        part = piece(k, PARTS_B)
        cp = remote(win.at[s, part], rbuf.at[n, part], br_s.at[n, k], br_r.at[n, k], to)
        cp.start()
        back[n, k] = cp

    def bsend_all(n, s, to):
        for k in range(PARTS_B):
            bsend(n, k, s, to)

    def badd(n, k, s):
        part = piece(k, PARTS_B)
        back[n, k].wait_recv()
        win[s, part] += rbuf[n, part]

    from_q, from_y = dev(q, yy, c), dev(x, yy + h, c)
    hq_to = (jnp.where(c == 0, from_q[0], from_y[0]), jnp.where(c == 0, from_q[1], from_y[1]))
    second_pass(s_ho)
    second_pass(s_hw)
    add_mate(s_ho)
    bsend_all(0, s_ho, dev(q, yy, c))
    second_pass(s_o)
    add_mate(s_hw)
    second_pass(s_lq)
    add_mate(s_o)
    bsend_all(1, s_o, dev(w, yy, c))
    second_pass(s_hq)
    add_mate(s_lq)
    bsend_all(2, s_lq, dev(x, yy + l, c))
    second_pass(s_q)
    add_mate(s_hq)
    bsend_all(3, s_hq, hq_to)
    aa_all().wait_recv()

    total = ar_a[0]
    for k in range(1, PLANE):
        total = total + ar_a[k]
    wg_sum[...] = total
    ar_b[zi] = total

    @pl.loop(1, nz)
    def _(d):
        ab_copy(d).start()


    def pass_on_hw(k):
        badd(0, k, s_hw)
        bsend(4, k, s_hw, dev(x, yy + h, c))

    pass_on_hw(0)
    second_pass(s_lx, whole=True)
    pass_on_hw(1)
    add_mate(s_q)
    second_pass(s_hx, whole=True)
    for k in range(2, PARTS_B):
        pass_on_hw(k)
    add_mate(s_lx)
    bsend_all(5, s_lx, dev(x, yy + l, c))
    second_pass(s_w, whole=True)
    ab_all().wait_recv()

    total = ar_b[0]
    for k in range(1, nz):
        total = total + ar_b[k]
    wg_all[m_me] = total

    @pl.loop(1, PLANE)
    def _(d):
        ac_copy(d).start()

    add_mate(s_hx)
    s_3 = jnp.where(c == 0, s_hx, s_q)

    def pass_on_q(k):
        badd(1, k, s_q)
        badd(2, k, s_q)
        badd(3, k, s_3)
        bsend(6, k, s_q, dev(q, yy, c))
        bsend(7, k, s_hx, dev(x, yy + h, c))

    def pass_on_w(k):
        badd(4, k, s_w)
        bsend(8, k, s_w, dev(w, yy, c))

    pass_on_q(0)
    second_pass(own, whole=True)
    add_mate(s_w)
    pass_on_w(0)
    for k in range(1, PARTS_B):
        pass_on_q(k)
        pass_on_w(k)
    add_mate(own)
    for k in range(PARTS_B):
        badd(5, k, own)

    ac_all().wait_recv()

    wg_cp = pltpu.make_async_copy(wg_all, wg_out, loc_sem.at[10])
    wg_cp.start()
    for cp in rs0 + rs1 + rs2 + ag:
        cp.wait_send()
    for i in range(WIN // 2):
        mate_copy(2 * i + 1 - c).wait_send()

    aa_all().wait_send()

    ab_all().wait_send()

    for n in range(6):
        for k in range(PARTS_B):
            back[n, k].wait_send()
    for k in range(PARTS_B):
        badd(6, k, own)
        badd(7, k, own)

    ac_all().wait_send()

    for n in (6, 7):
        for k in range(PARTS_B):
            back[n, k].wait_send()
    for k in range(PARTS_B):
        badd(8, k, own)
    rs_in[1] = win[own].T
    fg_cp = pltpu.make_async_copy(rs_in.at[1], fg_out, loc_sem.at[9])
    fg_cp.start()

    for k in range(PARTS_B):
        back[8, k].wait_send()

    act_cp.wait()
    fg_cp.wait()
    wg_cp.wait()


def shards(features, weight, cotangent, tile_row, tile_col, tile_count, tile_values):
    nz = lax.axis_size("row") // 8
    anywhere = pl.BlockSpec(memory_space=pl.ANY)
    sem = pltpu.SemaphoreType.DMA
    act, fg, wg = pl.pallas_call(
        kernel,
        out_shape=(
            pltpu.VMEM((ROWS, F), F32),
            pltpu.VMEM((ROWS, F), F32),
            pltpu.VMEM((PLANE, F // PLANE, F), F32),
        ),
        in_specs=[anywhere] * 7,
        out_specs=(anywhere,) * 3,
        scratch_shapes=[
            pltpu.VMEM((SLOTS, TILE, TILE), F32),
            pltpu.VMEM((SLOTS + 1, TILE, TILE), F32),
            pltpu.VMEM((WIN, TPB * TILE, 2 * TILE), BF16),
            pltpu.VMEM((WIN, TPB * TILE, 2 * TILE), BF16),
            pltpu.VMEM((WIN, ROWS, F), F32),
            pltpu.VMEM((4 * ROWS, F), F32),
            pltpu.VMEM((2, ROWS, F), F32),
            pltpu.VMEM((ROWS, F), F32),
            pltpu.VMEM((ROWS, F), F32),
            pltpu.VMEM((4, 2, F, HALF), F32),
            pltpu.VMEM((2, F, 2 * ROWS), BF16),
            pltpu.VMEM((2, F, 2 * ROWS), BF16),
            pltpu.VMEM((WIN // 2, F, ROWS), F32),
            pltpu.VMEM((9, F, ROWS), F32),
            pltpu.VMEM((PLANE, F // PLANE, F), F32),
            pltpu.VMEM((PLANE, F // PLANE, F), F32),
            pltpu.VMEM((nz, F // PLANE, F), F32),
            pltpu.VMEM((F // PLANE, F), F32),
            pltpu.VMEM((PLANE, F // PLANE, F), F32),
            pltpu.VMEM((ROWS, F), F32),
            pltpu.VMEM((F, F), F32),
            pltpu.VMEM((1, 1, SLOTS), jnp.int32),
            pltpu.VMEM((1, 1, SLOTS), jnp.int32),
            pltpu.VMEM((1, 1), jnp.int32),
            pltpu.VMEM((8, SLOTS), jnp.int32),
            pltpu.SMEM((8, SLOTS), jnp.int32),
            sem((11,)), sem((19, PARTS_F)), sem((WIN, PARTS_F)), sem((6,)), sem((6,)), sem((3, 2)), sem((4, 2)),
            sem((WIN // 2,)), sem((WIN // 2,)), sem((9, PARTS_B)), sem((9, PARTS_B)),
            *[sem] * 6,
        ],
        compiler_params=pltpu.CompilerParams(
            collective_id=0, has_side_effects=True, vmem_limit_bytes=62 * 1024 * 1024
        ),
    )(features, weight, cotangent, tile_values[0, 0], tile_row, tile_col, tile_count)
    return act, fg, wg.reshape(F, F)


def solution(mesh):
    placed = (
        P(("row", "rep"), None),
        P(),
        P(("row", "rep"), None),
        P("row", "rep", None),
        P("row", "rep", None),
        P("row", "rep"),
        P("row", "rep", None, None, None),
    )
    return jax.shard_map(
        shards,
        mesh=mesh,
        in_specs=placed,
        out_specs=(P(("row", "rep"), None), P(("row", "rep"), None), P()),
        check_vma=False,
    )
```

```python
import jax
import jax.numpy as jnp
from jax import lax
from jax.experimental import pallas as pl
from jax.experimental.pallas import tpu as pltpu
from jax.sharding import PartitionSpec as P

TILE = 128
TPB = 8
SPAN = 2
SLOTS = 128
F = 256
ROWS = 256
WIN = 20
BAND_TILES = 40
PLANE = 32
PARTS_F = 2
PARTS_B = 4
HALF = 128
MESH = pl.DeviceIdType.MESH
F32 = jnp.float32
BF16 = jnp.bfloat16


def split(value):
    high = value.astype(BF16)
    low = (value - high.astype(F32)).astype(BF16)
    return high, low


def dot(a, b):
    return jnp.dot(a, b, preferred_element_type=F32)


def dot_t(a, b):
    return lax.dot_general(a, b, (((1,), (1,)), ((), ())), preferred_element_type=F32)


def dot3(op, a, b):
    ah, al = split(a)
    bh, bl = split(b)
    return op(ah, bh) + (op(al, bh) + op(ah, bl))


def choose(i, values):
    out = values[0]
    for k in range(1, len(values)):
        out = jnp.where(i == k, values[k], out)
    return out


def plan_tiles(row, total_tiles, rows, cols, count, plan):
    sub = lax.broadcasted_iota(jnp.int32, (SLOTS, SLOTS), 0)
    lane = lax.broadcasted_iota(jnp.int32, (SLOTS, SLOTS), 1)
    line = lax.broadcasted_iota(jnp.int32, (1, SLOTS), 1)

    def total(mask_or_value):
        return jnp.sum(mask_or_value, axis=0, keepdims=True)

    def ones(mask):
        return jnp.where(mask, 1, 0)

    position = cols - (row - SPAN) * TPB
    position = jnp.where(position < 0, position + total_tiles, position)
    position = jnp.where(position >= total_tiles, position - total_tiles, position)
    key = jnp.where(line < count, rows * BAND_TILES + position, TPB * BAND_TILES + line)
    key_r = jnp.broadcast_to(key, (SLOTS, SLOTS))
    key_c = key_r.T
    twin = ones((key_c == key_r) & (sub < lane))
    rank = total(ones(key_c < key_r) + twin)
    again = jnp.minimum(total(twin), 1)
    code = jnp.broadcast_to(rank * 2 + again, (SLOTS, SLOTS)).T
    again_c = code & 1
    hit = code - again_c == lane * 2
    plan[0:1, :] = total(jnp.where(hit, sub, 0))
    plan[1:2, :] = total(jnp.where(hit, again_c, 0))
    for part in range(3):
        spot = lane + part * SLOTS
        upto = total(ones(key_c <= spot))
        there = total(ones(key_c == spot))
        plan[2 + part:3 + part, :] = jnp.where(there > 0, upto - 1, SLOTS)


def kernel(
    feat, weight, cot, tiles, tile_row, tile_col, tile_count,
    act_out, fg_out, wg_out,
    tilebuf, run, dense_h, dense_l, win, acc, rs_in, rs_mid, rs_send, gt, gt_h, gt_l, mrecv, rbuf,
    wg_loc, ar_a, ar_b, wg_sum, wg_all, cot_v, w_v, row_v, col_v, count_v, plan_v, plan,
    loc_sem, fs_sem, fr_sem, rs_s, rs_r, ag_s, ag_r, bm_s, bm_r, br_s, br_r,
    aa_s, aa_r, ab_s, ab_r, ac_s, ac_r,
):
    row = lax.axis_index("row")
    rep = lax.axis_index("rep")
    yy = lax.div(row, 2)
    xl = lax.div(rep, 2)
    c = lax.rem(rep, 2)
    xh = lax.rem(row, 2)
    x = xh * 2 + xl
    q = x + 1 - 2 * xl
    w = 3 - x
    o = lax.rem(x + 2, 4)
    h = 2 * xh - 1
    l = 1 - 2 * xh
    nyy = lax.axis_size("row") // 2

    def dev(xx, yv, cc):
        yv = lax.rem(yv + nyy, nyy)
        return (yv * 2 + lax.div(xx, 2), lax.rem(xx, 2) * 2 + cc)

    def slot(at, dyy, xx, cc):
        return (2 * dyy + lax.div(xx, 2) - lax.div(at, 2) + SPAN) * 4 + lax.rem(xx, 2) * 2 + cc

    mate = dev(x, yy, 1 - c)
    zi = lax.div(row, 8)
    nz = nyy // 4
    m_me = lax.rem(row, 8) * 4 + rep

    def plane_dev(m):
        return (zi * 8 + lax.div(m, 4), lax.rem(m, 4))

    def remote(src, dst, ssem, rsem, to):
        return pltpu.make_async_remote_copy(
            src_ref=src, dst_ref=dst, send_sem=ssem, recv_sem=rsem, device_id=to, device_id_type=MESH
        )

    tile_cp = pltpu.make_async_copy(tiles, tilebuf, loc_sem.at[0])
    tile_cp.start()
    own = slot(x, 0, x, c)
    feat_cp = pltpu.make_async_copy(feat, win.at[own], loc_sem.at[1])
    feat_cp.start()
    cot_cp = pltpu.make_async_copy(cot, cot_v, loc_sem.at[2])
    cot_cp.start()
    w_cp = pltpu.make_async_copy(weight, w_v, loc_sem.at[3])
    w_cp.start()
    list_cps = [
        pltpu.make_async_copy(src, dst, loc_sem.at[4 + i])
        for i, (src, dst) in enumerate(((tile_row, row_v), (tile_col, col_v), (tile_count, count_v)))
    ]
    for cp in list_cps:
        cp.start()

    bar = pltpu.get_barrier_semaphore()

    def greet(to):
        pl.semaphore_signal(bar, inc=1, device_id=to, device_id_type=MESH)

    @pl.loop(1, PLANE)
    def _(d):
        greet(plane_dev(lax.rem(m_me + d, PLANE)))

    @pl.loop(1, nz)
    def _(d):
        greet((lax.rem(row + 8 * d, nz * 8), rep))

    greet(dev(x, yy + 1, c))
    greet(dev(x, yy - 1, c))
    pl.semaphore_wait(bar, PLANE - 1 + nz - 1 + 2)

    sends = []

    def piece(k, parts):
        return pl.ds(k * (ROWS // parts), ROWS // parts)

    def fsend(n, k, src, dst_slot, to):
        part = piece(k, PARTS_F)
        cp = remote(src.at[part], win.at[dst_slot, part], fs_sem.at[n, k], fr_sem.at[dst_slot, k], to)
        cp.start()
        sends.append(cp)

    def frecv(s, k):
        part = piece(k, PARTS_F)
        remote(feat.at[part], win.at[s, part], fs_sem.at[0, k], fr_sem.at[s, k], mate).wait_recv()

    for k in range(PARTS_F):
        fsend(1, k, feat, slot(x, -1, x, c), dev(x, yy + 1, c))
        fsend(2, k, feat, slot(x, 1, x, c), dev(x, yy - 1, c))
        fsend(0, k, feat, slot(q, 0, x, c), dev(q, yy, c))
        fsend(3, k, feat, slot(w, 0, x, c), dev(w, yy, c))
    for k in range(PARTS_F):
        fsend(4, k, feat, own, mate)

    acc[...] = jnp.zeros_like(acc)
    run[SLOTS] = jnp.zeros((TILE, TILE), F32)
    for cp in list_cps:
        cp.wait()
    plan_tiles(row, nyy * 2 * TPB, row_v[0], col_v[0], count_v[...], plan_v)
    plan_cp = pltpu.make_async_copy(plan_v, plan, loc_sem.at[7])
    plan_cp.start()
    plan_cp.wait()
    tile_cp.wait()

    def merge(t, prev):
        value = prev * plan[1, t].astype(F32) + tilebuf[plan[0, t]]
        run[t] = value
        return value

    lax.fori_loop(0, SLOTS, merge, jnp.zeros((TILE, TILE), F32))

    feat_cp.wait()

    def forward(s):
        for r in range(TPB):
            for half in range(2):
                spot = s * 2 + (r * BAND_TILES + half)
                high, low = split(run[plan[2 + lax.div(spot, SLOTS), lax.rem(spot, SLOTS)]])
                dense_h[s, r * TILE:(r + 1) * TILE, half * TILE:(half + 1) * TILE] = high
                dense_l[s, r * TILE:(r + 1) * TILE, half * TILE:(half + 1) * TILE] = low
        xh_, xl_ = split(win[s])
        a = dense_h[s]
        acc[...] += dot(a, xh_) + (dot(dense_l[s], xh_) + dot(a, xl_))

    def forward_group(slots):
        @pl.loop(0, len(slots))
        def _(i):
            forward(choose(i, slots))

    def forward_recv_group(slots):
        @pl.loop(0, len(slots))
        def _(i):
            s = choose(i, slots)
            for k in range(PARTS_F):
                frecv(s, k)
            forward(s)

    def flip(s):
        return s + 1 - 2 * c

    s_q, s_w = slot(x, 0, q, c), slot(x, 0, w, c)
    s_hx, s_lx = slot(x, h, x, c), slot(x, l, x, c)
    s_o, s_hw = slot(x, 0, o, c), slot(x, h, w, c)
    s_lq, s_hq = slot(x, l, q, c), slot(x, h, q, c)
    s_ho = slot(x, h, o, c)

    qh_src = jnp.where(c == 0, s_hx, s_q)
    qh_dst = jnp.where(c == 0, slot(q, h, x, c), slot(x, h, q, c))
    to_q, to_y = dev(q, yy, c), dev(x, yy - h, c)
    qh_to = (jnp.where(c == 0, to_q[0], to_y[0]), jnp.where(c == 0, to_q[1], to_y[1]))

    def relay(n, k, s):
        frecv(s, k)
        fsend(n, k, win.at[s], s, mate)

    forward_group([own])
    for k in range(PARTS_F):
        frecv(s_w, k)
        fsend(7, k, win.at[s_w], slot(x, h, w, c), dev(x, yy - h, c))
        frecv(s_q, k)
        fsend(6, k, win.at[s_q], slot(x, l, q, c), dev(x, yy + h, c))
        fsend(5, k, win.at[s_q], slot(w, 0, q, c), dev(w, yy, c))
        frecv(s_hx, k)
        fsend(8, k, win.at[qh_src], qh_dst, qh_to)
        fsend(9, k, win.at[s_q], s_q, mate)
        fsend(10, k, win.at[s_w], s_w, mate)
        fsend(11, k, win.at[s_hx], s_hx, mate)
        relay(12, k, s_lx)
        if k == 0:
            forward_recv_group([flip(own)])
    forward_group([s_q, s_w, s_hx, s_lx])

    for k in range(PARTS_F):
        frecv(s_hw, k)
        fsend(13, k, win.at[s_hw], slot(q, h, w, c), dev(q, yy, c))
        fsend(14, k, win.at[s_hw], s_hw, mate)
        if k == 0:
            forward_recv_group([flip(s_q), flip(s_w)])
    forward_recv_group([flip(s_hx), flip(s_lx)])
    for k in range(PARTS_F):
        relay(15, k, s_o)
        relay(16, k, s_lq)
    forward_group([s_hw, s_o, s_lq])
    for k in range(PARTS_F):
        relay(17, k, s_hq)
    relay(18, 0, s_ho)
    forward_group([s_hq])
    forward_recv_group([flip(s_hw), flip(s_o), flip(s_lq)])
    for k in range(1, PARTS_F):
        relay(18, k, s_ho)
    forward_recv_group([flip(s_hq)])
    forward_group([s_ho])
    forward_recv_group([flip(s_ho)])

    k_o = (1 - xl) * 2 + c
    k_m = xl * 2 + 1 - c
    k_mo = (1 - xl) * 2 + 1 - c

    def chunk(k):
        return acc.at[pl.ds(pl.multiple_of(k * ROWS, ROWS), ROWS)]

    def half_of(k, n):
        return acc.at[pl.ds(pl.multiple_of(k * ROWS + n * HALF, HALF), HALF)]

    halves = [pl.ds(n * HALF, HALF) for n in range(2)]
    rs0 = [remote(half_of(k_mo, n), rs_in.at[0, halves[n]], rs_s.at[n], rs_r.at[n], mate) for n in range(2)]
    rs1 = [remote(half_of(k_m, n), rs_in.at[1, halves[n]], rs_s.at[2 + n], rs_r.at[2 + n], mate) for n in range(2)]
    rs2 = [remote(rs_send.at[halves[n]], rs_mid.at[halves[n]], rs_s.at[4 + n], rs_r.at[4 + n], dev(q, yy, c)) for n in range(2)]
    for cp in rs0 + rs1:
        cp.start()
    for cp in sends:
        cp.wait_send()
    for n in range(2):
        rs0[n].wait_recv()
        rs_send[halves[n]] = half_of(k_o, n)[...] + rs_in[0, halves[n]]
        rs2[n].start()
    cot_cp.wait()
    w_cp.wait()
    wh, wl = split(w_v[...])

    def gt_copy(k, n, number, to):
        return remote(gt.at[k, n], gt.at[k, n], ag_s.at[number, n], ag_r.at[k, n], to)

    def grecv(k, n):
        gt_copy(k, n, 0, mate).wait_recv()

    ag = []
    aggs, gps = [], []
    for n in range(2):
        rs1[n].wait_recv()
        part = half_of(rep, n)[...] + rs_in[1, halves[n]]
        rs2[n].wait_recv()
        agg = part + rs_mid[halves[n]]
        ah, al = split(agg)
        pre = dot(ah, wh) + (dot(al, wh) + dot(ah, wl))
        sig = jax.nn.sigmoid(pre)
        gp = cot_v[halves[n]] * (sig * (1.0 + pre * (1.0 - sig)))
        ph, plow = split(gp)
        gt[rep, n] = dot_t(wh, ph) + (dot_t(wl, ph) + dot_t(wh, plow))
        for number, to in ((0, dev(q, yy, c)), (1, mate)):
            cp = gt_copy(rep, n, number, to)
            cp.start()
            ag.append(cp)
        act_out[halves[n]] = pre * sig
        aggs.append(agg)
        gps.append(gp)
    agg = jnp.concatenate(aggs, axis=0)
    gp = jnp.concatenate(gps, axis=0)
    wg = dot3(dot, agg.T, gp).reshape(PLANE, F // PLANE, F)
    wg_loc[...] = wg

    def ar_copy(d, src, dst, ssem, rsem):
        return remote(src, dst, ssem, rsem, plane_dev(lax.rem(m_me + d, PLANE)))

    def aa_copy(d):
        return ar_copy(d, wg_loc.at[lax.rem(m_me + d, PLANE)], ar_a.at[m_me], aa_s, aa_r)

    def ab_copy(d):
        return remote(wg_sum, ar_b.at[zi], ab_s, ab_r, (lax.rem(row + 8 * d, nz * 8), rep))

    def ac_copy(d):
        return ar_copy(d, wg_all.at[m_me], wg_all.at[m_me], ac_s, ac_r)

    ar_a[m_me] = wg_loc[m_me]

    for n in range(2):
        grecv(k_m, n)

    def spread(pair):
        for core in range(2):
            for n in range(2):
                high, low = split(gt[pair * 2 + core, n])
                start = core * ROWS + n * HALF
                gt_h[pair, :, start:start + HALF] = high
                gt_l[pair, :, start:start + HALF] = low

    def backward(s, pair):
        rows = pl.ds(pl.multiple_of(pair * 2 * ROWS, 2 * ROWS), 2 * ROWS)
        a = dense_h[s, rows, :]
        g = gt_h[pair]
        return dot(g, a) + (dot(gt_l[pair], a) + dot(g, dense_l[s, rows, :]))

    spread(xl)

    def first_pass(slots):
        @pl.loop(0, len(slots))
        def _(i):
            s = choose(i, slots)
            win[s] = backward(s, xl)

    early = [s_ho, s_hw, s_o, s_lq, s_hq, s_q]
    early = [v for s in early for v in (flip(s), s)]
    first_pass(early[:4])
    for n in range(2):
        grecv(k_o, n)
        cp = gt_copy(k_o, n, 2, mate)
        cp.start()
        ag.append(cp)
        if n == 0:
            first_pass(early[4:10])
    def aa_all():
        some = pl.ds(0, PLANE - 1)
        return remote(wg_loc.at[some], ar_a.at[some], aa_s, aa_r, mate)

    def ab_all():
        some = pl.ds(0, nz - 1)
        return remote(ar_b.at[some], ar_b.at[some], ab_s, ab_r, mate)

    def ac_all():
        some = pl.ds(0, PLANE - 1)
        return remote(wg_all.at[some], wg_all.at[some], ac_s, ac_r, mate)

    @pl.loop(1, PLANE)
    def _(d):
        aa_copy(d).start()

    first_pass(early[10:])
    for n in range(2):
        grecv(k_mo, n)
    spread(1 - xl)

    def mate_copy(s):
        i = lax.div(s, 2)
        return remote(win.at[s], mrecv.at[i], bm_s.at[i], bm_r.at[i], mate)

    def second_pass(s, whole=False):
        @pl.loop(0, 2)
        def _(i):
            at = jnp.where(i == 0, flip(s), s)
            if whole:
                win[at] = backward(at, xl) + backward(at, 1 - xl)
            else:
                win[at] += backward(at, 1 - xl)

            @pl.when(i == 0)
            def _():
                mate_copy(at).start()

    def add_mate(s):
        mate_copy(s).wait_recv()
        win[s] += mrecv[lax.div(s, 2)]

    back = {}

    def bsend(n, k, s, to):
        part = piece(k, PARTS_B)
        cp = remote(win.at[s, part], rbuf.at[n, part], br_s.at[n, k], br_r.at[n, k], to)
        cp.start()
        back[n, k] = cp

    def bsend_all(n, s, to):
        for k in range(PARTS_B):
            bsend(n, k, s, to)

    def badd(n, k, s):
        part = piece(k, PARTS_B)
        back[n, k].wait_recv()
        win[s, part] += rbuf[n, part]

    from_q, from_y = dev(q, yy, c), dev(x, yy + h, c)
    hq_to = (jnp.where(c == 0, from_q[0], from_y[0]), jnp.where(c == 0, from_q[1], from_y[1]))
    second_pass(s_ho)
    second_pass(s_hw)
    add_mate(s_ho)
    bsend_all(0, s_ho, dev(q, yy, c))
    second_pass(s_o)
    add_mate(s_hw)
    second_pass(s_lq)
    add_mate(s_o)
    bsend_all(1, s_o, dev(w, yy, c))
    second_pass(s_hq)
    add_mate(s_lq)
    bsend_all(2, s_lq, dev(x, yy + l, c))
    second_pass(s_q)
    add_mate(s_hq)
    bsend_all(3, s_hq, hq_to)
    aa_all().wait_recv()

    total = ar_a[0]
    for k in range(1, PLANE):
        total = total + ar_a[k]
    wg_sum[...] = total
    ar_b[zi] = total

    @pl.loop(1, nz)
    def _(d):
        ab_copy(d).start()


    def pass_on_hw(k):
        badd(0, k, s_hw)
        bsend(4, k, s_hw, dev(x, yy + h, c))

    pass_on_hw(0)
    second_pass(s_lx, whole=True)
    pass_on_hw(1)
    add_mate(s_q)
    second_pass(s_hx, whole=True)
    for k in range(2, PARTS_B):
        pass_on_hw(k)
    add_mate(s_lx)
    bsend_all(5, s_lx, dev(x, yy + l, c))
    second_pass(s_w, whole=True)
    ab_all().wait_recv()

    total = ar_b[0]
    for k in range(1, nz):
        total = total + ar_b[k]
    wg_all[m_me] = total

    @pl.loop(1, PLANE)
    def _(d):
        ac_copy(d).start()

    add_mate(s_hx)
    s_3 = jnp.where(c == 0, s_hx, s_q)

    def pass_on_q(k):
        badd(1, k, s_q)
        badd(2, k, s_q)
        badd(3, k, s_3)
        bsend(6, k, s_q, dev(q, yy, c))
        bsend(7, k, s_hx, dev(x, yy + h, c))

    def pass_on_w(k):
        badd(4, k, s_w)
        bsend(8, k, s_w, dev(w, yy, c))

    pass_on_q(0)
    second_pass(own, whole=True)
    add_mate(s_w)
    pass_on_w(0)
    for k in range(1, PARTS_B):
        pass_on_q(k)
        pass_on_w(k)
    add_mate(own)
    for k in range(PARTS_B):
        badd(5, k, own)

    ac_all().wait_recv()

    wg_out[...] = wg_all[...]
    for cp in rs0 + rs1 + rs2 + ag:
        cp.wait_send()
    for i in range(WIN // 2):
        mate_copy(2 * i + 1 - c).wait_send()

    aa_all().wait_send()

    ab_all().wait_send()

    for n in range(6):
        for k in range(PARTS_B):
            back[n, k].wait_send()
    for k in range(PARTS_B):
        badd(6, k, own)
        badd(7, k, own)

    ac_all().wait_send()

    for n in (6, 7):
        for k in range(PARTS_B):
            back[n, k].wait_send()
    for k in range(PARTS_B):
        badd(8, k, own)
    fg_out[...] = win[own].T

    for k in range(PARTS_B):
        back[8, k].wait_send()


def shards(features, weight, cotangent, tile_row, tile_col, tile_count, tile_values):
    nz = lax.axis_size("row") // 8
    anywhere = pl.BlockSpec(memory_space=pl.ANY)
    sem = pltpu.SemaphoreType.DMA
    act, fg, wg = pl.pallas_call(
        kernel,
        out_shape=(
            pltpu.VMEM((ROWS, F), F32),
            pltpu.VMEM((ROWS, F), F32),
            pltpu.VMEM((PLANE, F // PLANE, F), F32),
        ),
        in_specs=[anywhere] * 7,
        out_specs=(pl.BlockSpec(memory_space=pltpu.VMEM),) * 3,
        scratch_shapes=[
            pltpu.VMEM((SLOTS, TILE, TILE), F32),
            pltpu.VMEM((SLOTS + 1, TILE, TILE), F32),
            pltpu.VMEM((WIN, TPB * TILE, 2 * TILE), BF16),
            pltpu.VMEM((WIN, TPB * TILE, 2 * TILE), BF16),
            pltpu.VMEM((WIN, ROWS, F), F32),
            pltpu.VMEM((4 * ROWS, F), F32),
            pltpu.VMEM((2, ROWS, F), F32),
            pltpu.VMEM((ROWS, F), F32),
            pltpu.VMEM((ROWS, F), F32),
            pltpu.VMEM((4, 2, F, HALF), F32),
            pltpu.VMEM((2, F, 2 * ROWS), BF16),
            pltpu.VMEM((2, F, 2 * ROWS), BF16),
            pltpu.VMEM((WIN // 2, F, ROWS), F32),
            pltpu.VMEM((9, F, ROWS), F32),
            pltpu.VMEM((PLANE, F // PLANE, F), F32),
            pltpu.VMEM((PLANE, F // PLANE, F), F32),
            pltpu.VMEM((nz, F // PLANE, F), F32),
            pltpu.VMEM((F // PLANE, F), F32),
            pltpu.VMEM((PLANE, F // PLANE, F), F32),
            pltpu.VMEM((ROWS, F), F32),
            pltpu.VMEM((F, F), F32),
            pltpu.VMEM((1, 1, SLOTS), jnp.int32),
            pltpu.VMEM((1, 1, SLOTS), jnp.int32),
            pltpu.VMEM((1, 1), jnp.int32),
            pltpu.VMEM((8, SLOTS), jnp.int32),
            pltpu.SMEM((8, SLOTS), jnp.int32),
            sem((8,)), sem((19, PARTS_F)), sem((WIN, PARTS_F)), sem((6,)), sem((6,)), sem((3, 2)), sem((4, 2)),
            sem((WIN // 2,)), sem((WIN // 2,)), sem((9, PARTS_B)), sem((9, PARTS_B)),
            *[sem] * 6,
        ],
        compiler_params=pltpu.CompilerParams(
            collective_id=0, has_side_effects=True, vmem_limit_bytes=62 * 1024 * 1024
        ),
    )(features, weight, cotangent, tile_values[0, 0], tile_row, tile_col, tile_count)
    return act, fg, wg.reshape(F, F)


def solution(mesh):
    placed = (
        P(("row", "rep"), None),
        P(),
        P(("row", "rep"), None),
        P("row", "rep", None),
        P("row", "rep", None),
        P("row", "rep"),
        P("row", "rep", None, None, None),
    )
    return jax.shard_map(
        shards,
        mesh=mesh,
        in_specs=placed,
        out_specs=(P(("row", "rep"), None), P(("row", "rep"), None), P()),
        check_vma=False,
    )
```
